512 devices in a mesh: lon: 64 (over y, z_lo, core), rad: 8 (over z_hi, x).
Axes of the slice: x: 4, y: 4, z: 16 (z_hi: 2, z_lo: 8; z = z_hi * 8 + z_lo), core: 2. Of those that a mesh axis runs over, the one named last changes fastest.
Arguments:
- logvisc: float32 [96, 256, 512], P('rad', 'lon'), may hold values from -1 to 1
- momentum: float32 [96, 256, 512], P('rad', 'lon'), may hold values from -6 to 6
- displacement: float32 [3, 96, 256, 512], P(None, 'rad', 'lon'), may hold values from -6 to 6
- ice_history: float32 [8, 256, 512], P(None, 'lon'), may hold values from -6 to 6
- load_steps: int32 [2], replicated, may hold values from 0 to 7
- site_cells: int32 [768], P('lon'), may hold values from 0 to 131071
- observed: float32 [3, 768], P(None, 'lon'), may hold values from -6 to 6
- site_weight: float32 [3, 768], P(None, 'lon'), may hold values from 2 to 6
Outputs:
- new_logvisc: float32 [96, 256, 512], P('rad', 'lon')
- half_momentum: float32 [96, 256, 512], P('rad', 'lon')
- misfit: float32 [1], replicated
The draws below stay inside these ranges and needn't reach their ends.
Inputs may be any that keep to these rules, and one draw needn't show every extreme that they name: site_cells holds lon * 512 + lat of the surface cell where the site stands. load_steps indexes the first dimension of ice_history.
All inputs are finite; a program needn't handle non-finite values.
Results may differ from the reference program's by a relative error of at most 0.0003.
Values sent between devices are 32-bit elements; how exact they have to be, the bound alone decides.
A program may use at most 64 MiB of HBM per device.

```python
import math
import jax
import jax.numpy as jnp
from jax import lax

NR = 96
NLAT = 512
SITES_DEV = 12
RELAX = 2
HIST = 8
NLON = 256
SITES = 768


def set_ends(array, own_key, least, high):
    extent = array.shape
    index_at = [jax.random.randint(jax.random.fold_in(own_key, axis), (), 0, extent[axis]) for axis in range(len(extent))]
    array = array.at[tuple(index_at)].set(least)
    longest = extent.index(max(extent))
    index_at[longest] = (index_at[longest] + 1) % extent[longest]
    return array.at[tuple(index_at)].set(high)


def steps_of(key, shape, split, low, largest):
    factor_of = 1.0
    for axis_at, shards_of in split:
        steps = jax.random.uniform(jax.random.fold_in(jax.random.fold_in(key, 6), axis_at), (shards_of,), jnp.float32, low / len(split), largest / len(split))
        factor_of = factor_of * jnp.repeat(jnp.exp(steps), shape[axis_at] // shards_of).reshape((-1,) + (1,) * (len(shape) - 1 - axis_at))
    return factor_of


def gaussian(key, dims, deviation, bound, pieces=(), held_as=jnp.bfloat16):
    entries = jax.random.normal(key, dims, jnp.float32) * deviation
    if len(pieces) > 0:
        entries = steps_of(key, dims, pieces, -0.22, 0.18) * entries
    return jnp.clip(entries, min=-bound, max=bound).astype(held_as)


def setup_inputs(seed: int = 0) -> dict:
    keys = jax.random.split(jax.random.key(seed), 9)
    return {
        "logvisc": jnp.clip(jax.random.uniform(keys[0], (NR, NLON, NLAT), jnp.float32, -1.0, 1.0) * steps_of(keys[0], (NR, NLON, NLAT), ((0, 8), (1, 64)), -0.4, 0.0), -1.0, 1.0),
        "momentum": gaussian(keys[1], (NR, NLON, NLAT), 1.0, 6.0, ((0, 8), (1, 64)), jnp.float32),
        "displacement": gaussian(keys[2], (3, NR, NLON, NLAT), 1.0, 6.0, ((1, 8), (2, 64)), jnp.float32),
        "ice_history": gaussian(keys[3], (HIST, NLON, NLAT), 1.0, 6.0, ((1, 64),), jnp.float32),
        "load_steps": jax.random.randint(keys[4], (RELAX,), 0, HIST).astype(jnp.int32),
        "site_cells": set_ends(jax.random.randint(keys[5], (SITES,), 0, NLON * NLAT), jax.random.fold_in(keys[5], 1), 0, (NLON * NLAT) - 1).astype(jnp.int32),
        "observed": gaussian(keys[6], (3, SITES), 1.0, 6.0, ((1, 64),), jnp.float32),
        "site_weight": jnp.clip(jnp.exp(math.log(6.0) - 1.0986123 * jax.random.uniform(keys[7], (3, SITES), jnp.float32) ** steps_of(keys[7], (3, SITES), ((1, 64),), -0.2, 0.2)), 2.0, 6.0),
    }


RELAX_RATE = 0.05
KERNEL_WIDTH = 0.1
KERNEL_WAVE = 40.0
PRIOR_WEIGHT = 0.1
LOAD_FACTOR = 1.0

def harmonic(center_fluid, other_fluid):
    summed = center_fluid + other_fluid
    coeff = 2.0 * center_fluid * other_fluid / summed
    slope = 2.0 * other_fluid * other_fluid / (summed * summed)
    return (coeff, slope)

def neighbours(padded):
    return [padded[:, 2:, 1:-1, 1:-1], padded[:, :-2, 1:-1, 1:-1], padded[:, 1:-1, 2:, 1:-1], padded[:, 1:-1, :-2, 1:-1], padded[:, 1:-1, 1:-1, 2:], padded[:, 1:-1, 1:-1, :-2]]

def middle(padded):
    return padded[:, 1:-1, 1:-1, 1:-1]

def apply_operator(field_pad, fluid_pad):
    fluid_mid = middle(fluid_pad)
    field_mid = middle(field_pad)
    total = jnp.zeros(field_mid.shape, jnp.float32)
    for fluid_side, field_side in zip(neighbours(fluid_pad), neighbours(field_pad)):
        coeff, slope = harmonic(fluid_mid, fluid_side)
        total = total + coeff * (field_side - field_mid)
    return total

def fluid_gradient(state_pad, adjoint_pad, fluid_pad):
    fluid_mid = middle(fluid_pad)
    state_mid = middle(state_pad)
    adjoint_mid = middle(adjoint_pad)
    total = jnp.zeros(fluid_mid.shape, jnp.float32)
    for fluid_side, state_side, adjoint_side in zip(neighbours(fluid_pad), neighbours(state_pad), neighbours(adjoint_pad)):
        coeff, slope = harmonic(fluid_mid, fluid_side)
        product = lax.optimization_barrier(jnp.sum((state_side - state_mid) * (adjoint_side - adjoint_mid), axis=0, keepdims=True))
        total = total + slope * product
    return -RELAX_RATE * total

def pad_whole(field):
    wrapped = jnp.concatenate([field[:, :, -1:], field, field[:, :, :1]], axis=2)
    return jnp.pad(wrapped, ((0, 0), (1, 1), (0, 0), (1, 1)))

def cell_features(lon_index, lat_index, total_lon, total_lat):
    theta = math.pi * (lat_index.astype(jnp.float32) + 0.5) / total_lat
    phi = 2.0 * math.pi * lon_index.astype(jnp.float32) / total_lon
    upward = jnp.broadcast_to(jnp.cos(theta)[None, :], (phi.shape[0], theta.shape[0]))
    eastern = jnp.sin(theta)[None, :] * jnp.cos(phi)[:, None]
    northern = jnp.sin(theta)[None, :] * jnp.sin(phi)[:, None]
    return jnp.stack([upward, eastern, northern]).reshape(3, -1)

def site_features(cells, total_lon, total_lat):
    lon_index = cells // total_lat
    lat_index = cells % total_lat
    theta = math.pi * (lat_index.astype(jnp.float32) + 0.5) / total_lat
    phi = 2.0 * math.pi * lon_index.astype(jnp.float32) / total_lon
    return jnp.stack([jnp.cos(theta), jnp.sin(theta) * jnp.cos(phi), jnp.sin(theta) * jnp.sin(phi)], axis=1)

def kernel(site_feats, cell_feats):
    cosine = site_feats[:, 0:1] * cell_feats[0:1] + site_feats[:, 1:2] * cell_feats[1:2] + site_feats[:, 2:3] * cell_feats[2:3]
    chord = 2.0 - 2.0 * cosine
    return 1.0 / (1.0 + chord / KERNEL_WIDTH) + 0.5 * jnp.cos(KERNEL_WAVE * chord)

def reference(logvisc, momentum, displacement, ice_history, load_steps, site_cells, observed, site_weight):
    fluidity = jnp.exp(-logvisc)
    fluid_pad = pad_whole(fluidity[None])
    radial = jnp.arange(NR).astype(jnp.float32)
    depth_weight = jnp.exp(4.0 * (radial - (NR - 1)) / NR)
    top_row = (jnp.arange(NR) == NR - 1).astype(jnp.float32)[None, :, None, None]
    upward = (jnp.arange(3) == 0).astype(jnp.float32)[:, None, None, None]
    state = displacement
    saved = []
    for level in range(RELAX):
        saved.append(state)
        padded = pad_whole(state)
        load = lax.dynamic_index_in_dim(ice_history, load_steps[level], 0, keepdims=False)
        state = state + RELAX_RATE * apply_operator(padded, fluid_pad) - LOAD_FACTOR * upward * top_row * load[None, None]
    surface = lax.optimization_barrier(jnp.sum(depth_weight[None, :, None, None] * state, axis=1)).reshape(3, -1)
    scale = 1.0 / math.sqrt(NLON * NLAT)
    cells_all = cell_features(jnp.arange(NLON), jnp.arange(NLAT), NLON, NLAT)
    feats = site_features(site_cells, NLON, NLAT)
    blocks = feats.reshape(-1, SITES_DEV, 3)

    def predict_block(block):
        weights = kernel(block, cells_all)
        return jnp.einsum('sm,cm->sc', weights, surface, precision=lax.Precision.HIGHEST, preferred_element_type=jnp.float32)
    predicted = (lax.map(predict_block, blocks).reshape(-1, 3) * scale).T
    weighted = site_weight * (predicted - observed)
    misfit = jnp.sum(weighted * weighted) / (3 * SITES)
    pulled = (site_weight * weighted).T.reshape(-1, SITES_DEV, 3)

    def spread_block(total, item):
        block, values = item
        weights = kernel(block, cells_all)
        return (total + jnp.einsum('sc,sm->cm', values, weights, precision=lax.Precision.HIGHEST, preferred_element_type=jnp.float32), None)
    summed, unused = lax.scan(spread_block, jnp.zeros((3, NLON * NLAT), jnp.float32), (blocks, pulled))
    surface_adjoint = (summed * scale).reshape(3, NLON, NLAT)
    adjoint = depth_weight[None, :, None, None] * surface_adjoint[:, None]
    gradient_fluid = jnp.zeros((1, NR, NLON, NLAT), jnp.float32)
    for level in range(RELAX - 1, -1, -1):
        adjoint_pad = pad_whole(adjoint)
        gradient_fluid = gradient_fluid + fluid_gradient(pad_whole(saved[level]), adjoint_pad, fluid_pad)
        if level > 0:
            adjoint = adjoint + RELAX_RATE * apply_operator(adjoint_pad, fluid_pad)
    gradient = -fluidity * gradient_fluid[0] + PRIOR_WEIGHT * logvisc
    half_momentum = momentum - 0.5 * gradient
    new_logvisc = logvisc + half_momentum
    return (new_logvisc, half_momentum, misfit.reshape(1))
```

```python
import functools
import math

import jax
import jax.numpy as jnp
from jax import lax
from jax.experimental import pallas as pl
from jax.experimental.pallas import tpu as pltpu
from jax.sharding import PartitionSpec as P

MESH = pl.DeviceIdType.MESH
NR, NLON, NLAT = 96, 256, 512
ROWS = 12
COLS = 4
SCALE = 1.0 / math.sqrt(NLON * NLAT)
WAVE = [0.5 * (-1) ** k * (2.0 * math.pi) ** (2 * k + 1) / math.factorial(2 * k + 1) for k in range(6)]


def place():
    lon, rad = lax.axis_index("lon"), lax.axis_index("rad")
    return lon // 16, (rad // 4) * 8 + (lon // 2) % 8, lon % 2, rad % 4


def device(y, z, c, x):
    return (y * 16 + (z % 8) * 2 + c, (z // 8) * 4 + x)


def z_peer(i):
    y, z, c, x = place()
    z2 = (z + i) % 16
    return device(y, z2, c, x), z2


def plane_peer(i):
    y, z, c, x = place()
    x2, y2, c2 = (x + i % 4) % 4, (y + (i // 4) % 4) % 4, (c + i // 16) % 2
    return device(y2, z, c2, x2), x2, y2 * 2 + c2


def block_peer(i):
    y, z, c, x = place()
    y2, c2 = (y + i % 4) % 4, (c + i // 4) % 2
    return device(y2, z, c2, x), y2 * 2 + c2


def x_peer(i):
    y, z, c, x = place()
    x2 = (x + i) % 4
    return device(y, z, c, x2), x2


def repeat(first, last, step):
    def one(i, carry):
        step(i)
        return carry

    lax.fori_loop(first, last, one, 0)


def send(src, dst, ssem, rsem, target):
    pltpu.make_async_remote_copy(
        src_ref=src, dst_ref=dst, send_sem=ssem, recv_sem=rsem, device_id=target, device_id_type=MESH
    ).start()


def await_bytes(ref, sem):
    pltpu.make_async_copy(ref, ref, sem).wait()


def iota(shape, dim):
    return lax.broadcasted_iota(jnp.int32, shape, dim)


def next_lat(v):
    return pltpu.roll(v, NLAT - 1, v.ndim - 1)


def last_lat(v):
    return pltpu.roll(v, 1, v.ndim - 1)


def next_row(v):
    return pltpu.roll(v, 15, 0)


def last_row(v):
    return pltpu.roll(v, 1, 0)


def blocks_to_lanes(blocks):
    lane = iota((8, 128), 1)
    tiles = []
    for t in range(6):
        b = (128 * t) // 96
        first, second = 96 * b - 128 * t, 96 * (b + 1) - 128 * t
        low = pltpu.roll(blocks[b], first % 128, 1) if first % 128 else blocks[b]
        high = pltpu.roll(blocks[b + 1], second % 128, 1)
        tiles.append(jnp.where(lane < second, low, high))
    return tiles


def lanes_to_blocks(tiles):
    lane = iota((8, 128), 1)
    blocks = []
    for b in range(8):
        t, offset = (96 * b) // 128, (96 * b) % 128
        block = pltpu.roll(tiles[t], 128 - offset, 1) if offset else tiles[t]
        if offset > 32:
            block = jnp.where(lane < 128 - offset, block, pltpu.roll(tiles[t + 1], 128 - offset, 1))
        blocks.append(jnp.where(lane < 96, block, 0.0))
    return blocks


def split(v):
    high = v.astype(jnp.bfloat16)
    return high, (v - high.astype(jnp.float32)).astype(jnp.bfloat16)


def kernel(
    lv_ref, u_ref, ice_ref, steps_ref, cells_ref, observed_ref, weight_ref,
    grad_ref, misfit_ref,
    X, E, S1, QA, QO, QR, radS, radR, lvS, lvR,
    packet, gathered, block, sites, SB, RB, KH, KL,
    PB, C1R, C2S, C2R, C3S, C3R, SD, DR, ssem, rsem,
):
    lon, rad = lax.axis_index("lon"), lax.axis_index("rad")
    y, z, c, x = place()
    own_block = y * 2 + c
    right, left = ((lon + 1) % 64, rad), ((lon + 63) % 64, rad)
    above, below = (lon, (rad + 1) % 8), (lon, (rad + 7) % 8)

    barrier = pltpu.get_barrier_semaphore()

    def greet(target):
        pl.semaphore_signal(barrier, 1, device_id=target, device_id_type=MESH)

    for target in (right, left, above, below):
        greet(target)
    repeat(1, 16, lambda i: greet(z_peer(i)[0]))
    repeat(1, 32, lambda i: greet(plane_peer(i)[0]))

    for f in range(4):
        for l in range(COLS):
            source = lv_ref[:, l, :] if f == 0 else u_ref[f - 1, :, l, :]
            X[f, l + 2, 0:ROWS, :] = source
            X[f, l + 2, ROWS:16, :] = jnp.zeros((16 - ROWS, NLAT), jnp.float32)
            radS[0, f * 4 + l : f * 4 + l + 1, :] = source[11:12, :]
            radS[1, f * 4 + l : f * 4 + l + 1, :] = source[0:1, :]
    packet[...] = jnp.zeros((8, 128), jnp.float32)
    packet[0:1, 0:12] = cells_ref[...].astype(jnp.float32)
    packet[1:4, 0:12] = observed_ref[...]
    packet[4:7, 0:12] = weight_ref[...]
    gathered[z % 8] = packet[...]

    pl.semaphore_wait(barrier, 50)

    send(radS.at[0], radR.at[0], ssem.at[0], rsem.at[0], above)
    send(radS.at[1], radR.at[1], ssem.at[1], rsem.at[1], below)
    send(X.at[:, 5], X.at[:, 1], ssem.at[2], rsem.at[2], right)
    send(X.at[:, 2], X.at[:, 6], ssem.at[3], rsem.at[3], left)

    def send_record(i):
        target, unused = z_peer((i + 12) % 16)
        send(packet, gathered.at[z % 8], ssem.at[4], rsem.at[4], target)

    repeat(0, 4, send_record)
    repeat(5, 8, send_record)

    row = iota((16, NLAT), 0)
    layer = jnp.where(row >= 14, row - 16, row)
    depth = (layer + rad * ROWS).astype(jnp.float32)
    wr = jnp.exp(4.0 * (depth - (NR - 1)) / NR)
    wr_next = jnp.exp(4.0 * (depth + 1.0 - (NR - 1)) / NR)
    own_row = row < ROWS
    wr_own = jnp.where(own_row, wr, 0.0)
    deep = layer + rad * ROWS
    face_ok = (row != 13) & (deep >= 0) & (deep < NR - 1)
    not_last = iota((16, NLAT), 1) < NLAT - 1
    is_top = jnp.where(rad == 7, 1.0, 0.0)

    await_bytes(gathered.at[pl.ds(0, 7)], rsem.at[4])
    record = gathered[0]
    for slot in range(1, 8):
        record = record + pltpu.roll(gathered[slot], 12 * slot, 1)
    block[...] = record
    sites[own_block] = record

    def send_block(i):
        target, unused = block_peer(i)
        send(block, sites.at[own_block], ssem.at[5], rsem.at[5], target)

    repeat(1, 8, send_block)

    await_bytes(radR.at[0], rsem.at[0])
    await_bytes(radR.at[1], rsem.at[1])
    await_bytes(X.at[:, 1], rsem.at[2])
    await_bytes(X.at[:, 6], rsem.at[3])
    await_bytes(X.at[:, 5], ssem.at[2])
    await_bytes(X.at[:, 2], ssem.at[3])
    for f in range(4):
        for l in range(COLS):
            X[f, l + 2, 15:16, :] = radR[0, f * 4 + l : f * 4 + l + 1, :]
            X[f, l + 2, 12:13, :] = radR[1, f * 4 + l : f * 4 + l + 1, :]

    def edge_lat(e):
        return jnp.where(not_last, 0.1 / (e + next_lat(e)), 0.0)

    def edge_rad(e):
        return jnp.where(face_ok, 0.1 / (e + next_row(e)), 0.0)

    for p in range(1, 7):
        E[p] = jnp.exp(X[0, p])
    for p in range(2, 6):
        QA[p] = edge_lat(E[p])
        QR[p] = edge_rad(E[p])
    for p in range(1, 6):
        QO[p] = 0.1 / (E[p] + E[p + 1])
    load_1, load_2 = ice_ref[steps_ref[0]], ice_ref[steps_ref[1]]
    for f in range(3):
        for p in range(2, 6):
            u = X[f + 1, p]
            flux = QA[p] * (next_lat(u) - u)
            rise = QR[p] * (next_row(u) - u)
            total = u + (flux - last_lat(flux)) + (rise - last_row(rise))
            total = total + QO[p] * (X[f + 1, p + 1] - u) + QO[p - 1] * (X[f + 1, p - 1] - u)
            if f == 0:
                pressed = jnp.broadcast_to(load_1[p - 2 : p - 1, :], (16, NLAT)) * is_top
                total = total - jnp.where(row == ROWS - 1, pressed, 0.0)
            S1[f, p] = total

    columns = []
    for f in range(3):
        columns.append([jnp.zeros((1, NLAT), jnp.float32) for unused in range(8)])

    def column_sum(v):
        return jnp.sum(v, axis=0, keepdims=True)

    for p in range(2, 6):
        slope = QR[p] * (wr_next - wr)
        factor = jnp.where(own_row, wr + slope - last_row(slope), 0.0)
        along = wr_own * QA[p]
        for f in range(3):
            s = S1[f, p]
            flux = column_sum(along * (next_lat(s) - s))
            columns[f][p] = columns[f][p] + column_sum(factor * s) + (flux - last_lat(flux))
    for p in range(1, 6):
        across = wr_own * QO[p]
        for f in range(3):
            if p == 1:
                flow = column_sum(across * S1[f, 2])
            elif p == 5:
                flow = -column_sum(across * S1[f, 5])
            else:
                flow = column_sum(across * (S1[f, p + 1] - S1[f, p]))
            columns[f][p] = columns[f][p] + flow
            columns[f][p + 1] = columns[f][p + 1] - flow
    for p in range(2, 6):
        columns[0][p] = columns[0][p] - load_2[p - 2 : p - 1, :] * is_top
    for f in range(3):
        for p in range(8):
            for band in range(4):
                SB[band, f * 8 + p : f * 8 + p + 1, :] = columns[f][p][:, band * 128 : band * 128 + 128]
    RB[x] = SB[x]

    def send_band(i):
        target, x2 = x_peer(i)
        send(SB.at[x2], RB.at[x], ssem.at[6], rsem.at[6], target)

    repeat(1, 4, send_band)

    for f in range(3):
        for l in range(COLS):
            radS[2, f * 4 + l : f * 4 + l + 1, :] = S1[f, l + 2, 11:12, :]
            radS[3, f * 4 + l : f * 4 + l + 1, :] = S1[f, l + 2, 0:1, :]
    for l in range(COLS):
        radS[2, 12 + l : 13 + l, :] = X[0, l + 2, 10:11, :]
        radS[3, 12 + l : 13 + l, :] = X[0, l + 2, 1:2, :]
    lvS[0] = jnp.where(own_row, X[0, 4], X[0, 5])
    lvS[1] = jnp.where(own_row, X[0, 3], X[0, 2])
    send(radS.at[2], radR.at[2], ssem.at[7], rsem.at[7], above)
    send(radS.at[3], radR.at[3], ssem.at[8], rsem.at[8], below)
    send(S1.at[:, 5], S1.at[:, 1], ssem.at[9], rsem.at[9], right)
    send(S1.at[:, 2], S1.at[:, 6], ssem.at[10], rsem.at[10], left)
    send(lvS.at[0], lvR.at[0], ssem.at[11], rsem.at[11], right)
    send(lvS.at[1], lvR.at[1], ssem.at[12], rsem.at[12], left)

    await_bytes(sites.at[pl.ds(0, 7)], rsem.at[5])
    tiles = blocks_to_lanes([sites[b] for b in range(8)])
    theta = (iota((128, 128), 0) + x * 128).astype(jnp.float32)
    theta = math.pi * (theta + 0.5) / NLAT
    cell_cos, cell_sin = jnp.cos(theta), jnp.sin(theta)
    plane_lon = (iota((8, 128), 0) + (lon * COLS - 2)).astype(jnp.float32)
    for t in range(6):
        cell = jnp.broadcast_to(tiles[t][0:1, :], (8, 128))
        site_lon = jnp.floor(cell * (1.0 / NLAT))
        site_theta = math.pi * (cell - NLAT * site_lon + 0.5) / NLAT
        up = jnp.cos(site_theta)
        side = jnp.sin(site_theta) * jnp.cos(2.0 * math.pi * (site_lon - plane_lon) / NLON)
        for p in range(8):
            cosine = cell_cos * up[0:1, :] + cell_sin * side[p : p + 1, :]
            chord = 2.0 - 2.0 * cosine
            turns = chord * (40.0 / (2.0 * math.pi))
            turns = 0.25 - jnp.abs(turns - jnp.round(turns))
            squared = turns * turns
            wave = jnp.full_like(squared, WAVE[5])
            for k in range(4, -1, -1):
                wave = wave * squared + WAVE[k]
            value = 1.0 / (1.0 + chord * 10.0) + wave * turns
            high, low = split(value)
            KH[p * 128 : p * 128 + 128, t * 128 : t * 128 + 128] = high
            KL[p * 128 : p * 128 + 128, t * 128 : t * 128 + 128] = low

    await_bytes(RB.at[pl.ds(0, 3)], rsem.at[6])
    band = (RB[0] + RB[1]) + (RB[2] + RB[3])
    place_of = iota((24, 128), 0) % 8
    wide = jnp.concatenate([jnp.where(place_of == p, band, 0.0) for p in range(8)], axis=1)
    high, low = split(wide)
    dot = functools.partial(jnp.dot, preferred_element_type=jnp.float32)
    parts = dot(high, KH[...]) + dot(high, KL[...]) + dot(low, KH[...])
    row8 = iota((8, 6 * 128), 0)
    pred = jnp.zeros((8, 6 * 128), jnp.float32)
    for f in range(3):
        summed = jnp.sum(parts[f * 8 : f * 8 + 8, :], axis=0, keepdims=True) * SCALE
        pred = jnp.where(row8 == f, jnp.broadcast_to(summed, pred.shape), pred)
    pieces = lanes_to_blocks([pred[:, t * 128 : t * 128 + 128] for t in range(6)])
    for b in range(8):
        PB[b] = pieces[b]
    C1R[x * 8 + own_block] = PB[own_block]

    def send_piece(i):
        target, unused, b2 = plane_peer(i)
        send(PB.at[b2], C1R.at[x * 8 + own_block], ssem.at[13], rsem.at[13], target)

    repeat(1, 32, send_piece)
    await_bytes(C1R.at[pl.ds(0, 31)], rsem.at[13])
    summed = jnp.sum(C1R[...], axis=0)
    C2S[...] = summed
    C2R[z] = summed

    def send_sum(i):
        target, unused = z_peer(i)
        send(C2S, C2R.at[z], ssem.at[14], rsem.at[14], target)

    repeat(1, 16, send_sum)

    await_bytes(radR.at[2], rsem.at[7])
    await_bytes(radR.at[3], rsem.at[8])
    await_bytes(S1.at[:, 1], rsem.at[9])
    await_bytes(S1.at[:, 6], rsem.at[10])
    await_bytes(lvR.at[0], rsem.at[11])
    await_bytes(lvR.at[1], rsem.at[12])
    await_bytes(S1.at[:, 5], ssem.at[9])
    await_bytes(S1.at[:, 2], ssem.at[10])
    for f in range(3):
        for l in range(COLS):
            S1[f, l + 2, 15:16, :] = radR[2, f * 4 + l : f * 4 + l + 1, :]
            S1[f, l + 2, 12:13, :] = radR[3, f * 4 + l : f * 4 + l + 1, :]
    for l in range(COLS):
        X[0, l + 2, 14:15, :] = radR[2, 12 + l : 13 + l, :]
        X[0, l + 2, 13:14, :] = radR[3, 12 + l : 13 + l, :]
    for side, far, near in ((0, 0, 1), (1, 7, 6)):
        X[0, far] = lvR[side]
        X[0, near] = jnp.where(own_row, X[0, near], lvR[side])
    for p in range(8):
        E[p] = jnp.exp(X[0, p])
    for p in range(1, 7):
        QA[p] = edge_lat(E[p])
        QR[p] = edge_rad(E[p])
    for p in range(7):
        QO[p] = 0.1 / (E[p] + E[p + 1])

    await_bytes(C2R.at[pl.ds(0, 15)], rsem.at[14])
    predicted = jnp.sum(C2R[...], axis=0)
    record = block[...]
    row_of, lane_of = iota((8, 128), 0), iota((8, 128), 1)
    entry = (row_of < 3) & (lane_of < 96)
    weight = jnp.where(entry, pltpu.roll(record, 4, 0), 0.0)
    weighted = weight * (predicted - pltpu.roll(record, 7, 0))
    squares = jnp.broadcast_to(jnp.sum(weighted * weighted, axis=0, keepdims=True), (8, 128))
    pulled = jnp.where(row_of == 3, squares, weight * weighted)
    C3S[...] = pulled
    C3R[own_block] = pulled

    def send_pulled(i):
        target, unused = block_peer(i)
        send(C3S, C3R.at[own_block], ssem.at[15], rsem.at[15], target)

    repeat(1, 8, send_pulled)
    await_bytes(C3R.at[pl.ds(0, 7)], rsem.at[15])
    pulls = [C3R[b] for b in range(8)]
    total = pulls[0]
    for b in range(1, 8):
        total = total + pulls[b]
    misfit_ref[0] = jnp.sum(total[3:4, :]) / (3.0 * 768.0)
    pull = jnp.concatenate(blocks_to_lanes(pulls), axis=1)
    high, low = split(pull)
    both = jnp.concatenate([high, low], axis=0)

    def against(lhs, rhs):
        return lax.dot_general(lhs, rhs, (((1,), (1,)), ((), ())), preferred_element_type=jnp.float32)

    first = against(both, KH[...])
    adjoint = (first[0:8] + first[8:16] + against(both, KL[...])[0:8]) * SCALE
    SD[...] = adjoint
    DR[x] = adjoint

    def send_adjoint(i):
        target, unused = x_peer(i)
        send(SD, DR.at[x], ssem.at[16], rsem.at[16], target)

    repeat(1, 4, send_adjoint)
    await_bytes(DR.at[pl.ds(0, 3)], rsem.at[16])

    faces_a = [jnp.zeros((16, NLAT), jnp.float32) for unused in range(8)]
    faces_r = [jnp.zeros((16, NLAT), jnp.float32) for unused in range(8)]
    faces_o = [jnp.zeros((16, NLAT), jnp.float32) for unused in range(8)]
    for f in range(3):
        a2 = []
        for p in range(8):
            surface = jnp.concatenate(
                [DR[band, f : f + 1, p * 128 : p * 128 + 128] for band in range(4)], axis=1
            )
            a2.append(wr * jnp.broadcast_to(surface, (16, NLAT)))
        a1 = [None] * 8
        for p in range(1, 7):
            flux = QA[p] * (next_lat(a2[p]) - a2[p])
            rise = QR[p] * (next_row(a2[p]) - a2[p])
            a1[p] = (
                a2[p] + (flux - last_lat(flux)) + (rise - last_row(rise))
                + QO[p] * (a2[p + 1] - a2[p]) + QO[p - 1] * (a2[p - 1] - a2[p])
            )
        for p in range(1, 6):
            u, s = X[f + 1, p], S1[f, p]
            faces_o[p] = (
                faces_o[p]
                + (X[f + 1, p + 1] - u) * (a1[p + 1] - a1[p])
                + (S1[f, p + 1] - s) * (a2[p + 1] - a2[p])
            )
            if p > 1:
                faces_a[p] = (
                    faces_a[p]
                    + (next_lat(u) - u) * (next_lat(a1[p]) - a1[p])
                    + (next_lat(s) - s) * (next_lat(a2[p]) - a2[p])
                )
                faces_r[p] = (
                    faces_r[p]
                    + (next_row(u) - u) * (next_row(a1[p]) - a1[p])
                    + (next_row(s) - s) * (next_row(a2[p]) - a2[p])
                )
    for p in range(1, 6):
        faces_o[p] = QO[p] * QO[p] * faces_o[p]
    for p in range(2, 6):
        along = QA[p] * QA[p] * faces_a[p]
        upward = QR[p] * QR[p] * faces_r[p]
        whole = (along + last_lat(along)) + (upward + last_row(upward)) + (faces_o[p] + faces_o[p - 1])
        result = 10.0 * E[p] * whole + 0.1 * X[0, p]
        grad_ref[:, p - 2, :] = result[0:ROWS, :]

    for k, ref in ((0, radS.at[0]), (1, radS.at[1]), (4, gathered.at[pl.ds(0, 7)]), (5, sites.at[pl.ds(0, 7)]), (6, RB.at[pl.ds(0, 3)]),
                   (7, radS.at[2]), (8, radS.at[3]), (11, lvS.at[0]),
                   (12, lvS.at[1]), (13, C1R.at[pl.ds(0, 31)]), (14, C2R.at[pl.ds(0, 15)]),
                   (15, C3R.at[pl.ds(0, 7)]), (16, DR.at[pl.ds(0, 3)])):
        await_bytes(ref, ssem.at[k])


def body(logvisc, momentum, displacement, ice_history, load_steps, site_cells, observed, site_weight):
    f32 = jnp.float32
    vmem = pl.BlockSpec(memory_space=pltpu.VMEM)
    smem = pl.BlockSpec(memory_space=pltpu.SMEM)
    gradient, misfit = pl.pallas_call(
        kernel,
        out_shape=(
            jax.ShapeDtypeStruct((ROWS, COLS, NLAT), f32),
            jax.ShapeDtypeStruct((1,), f32),
        ),
        in_specs=[vmem, vmem, vmem, smem, vmem, vmem, vmem],
        out_specs=(vmem, smem),
        scratch_shapes=[
            pltpu.VMEM((4, 8, 16, NLAT), f32),
            pltpu.VMEM((8, 16, NLAT), f32),
            pltpu.VMEM((3, 8, 16, NLAT), f32),
            pltpu.VMEM((8, 16, NLAT), f32),
            pltpu.VMEM((8, 16, NLAT), f32),
            pltpu.VMEM((8, 16, NLAT), f32),
            pltpu.VMEM((4, 16, NLAT), f32),
            pltpu.VMEM((4, 16, NLAT), f32),
            pltpu.VMEM((2, 16, NLAT), f32),
            pltpu.VMEM((2, 16, NLAT), f32),
            pltpu.VMEM((8, 128), f32),
            pltpu.VMEM((8, 8, 128), f32),
            pltpu.VMEM((8, 128), f32),
            pltpu.VMEM((8, 8, 128), f32),
            pltpu.VMEM((4, 24, 128), f32),
            pltpu.VMEM((4, 24, 128), f32),
            pltpu.VMEM((1024, 768), jnp.bfloat16),
            pltpu.VMEM((1024, 768), jnp.bfloat16),
            pltpu.VMEM((8, 8, 128), f32),
            pltpu.VMEM((32, 8, 128), f32),
            pltpu.VMEM((8, 128), f32),
            pltpu.VMEM((16, 8, 128), f32),
            pltpu.VMEM((8, 128), f32),
            pltpu.VMEM((8, 8, 128), f32),
            pltpu.VMEM((8, 1024), f32),
            pltpu.VMEM((4, 8, 1024), f32),
            pltpu.SemaphoreType.DMA((17,)),
            pltpu.SemaphoreType.DMA((17,)),
        ],
        compiler_params=pltpu.CompilerParams(
            collective_id=0, has_side_effects=True, vmem_limit_bytes=48 * 1024 * 1024
        ),
    )(logvisc, displacement, ice_history, load_steps, site_cells.reshape(1, 12), observed, site_weight)
    half_momentum = momentum - 0.5 * gradient
    return logvisc + half_momentum, half_momentum, misfit


def solution(mesh):
    return jax.shard_map(
        body,
        mesh=mesh,
        in_specs=(
            P("rad", "lon", None),
            P("rad", "lon", None),
            P(None, "rad", "lon", None),
            P(None, "lon", None),
            P(),
            P("lon"),
            P(None, "lon"),
            P(None, "lon"),
        ),
        out_specs=(P("rad", "lon", None), P("rad", "lon", None), P()),
        check_vma=False,
    )
```

```python
import functools
import math

import jax
import jax.numpy as jnp
from jax import lax
from jax.experimental import pallas as pl
from jax.experimental.pallas import tpu as pltpu
from jax.sharding import PartitionSpec as P

MESH = pl.DeviceIdType.MESH
NR, NLON, NLAT = 96, 256, 512
ROWS = 12
COLS = 4
SCALE = 1.0 / math.sqrt(NLON * NLAT)
WAVE = [0.5 * (-1) ** k * (2.0 * math.pi) ** (2 * k + 1) / math.factorial(2 * k + 1) for k in range(6)]


def place():
    lon, rad = lax.axis_index("lon"), lax.axis_index("rad")
    return lon // 16, (rad // 4) * 8 + (lon // 2) % 8, lon % 2, rad % 4


def device(y, z, c, x):
    return (y * 16 + (z % 8) * 2 + c, (z // 8) * 4 + x)


def z_peer(i):
    y, z, c, x = place()
    z2 = (z + i) % 16
    return device(y, z2, c, x), z2


def plane_peer(i):
    y, z, c, x = place()
    x2, y2, c2 = (x + i % 4) % 4, (y + (i // 4) % 4) % 4, (c + i // 16) % 2
    return device(y2, z, c2, x2), x2, y2 * 2 + c2


def block_peer(i):
    y, z, c, x = place()
    y2, c2 = (y + i % 4) % 4, (c + i // 4) % 2
    return device(y2, z, c2, x), y2 * 2 + c2


def x_peer(i):
    y, z, c, x = place()
    x2 = (x + i) % 4
    return device(y, z, c, x2), x2


def repeat(first, last, step):
    def one(i, carry):
        step(i)
        return carry

    lax.fori_loop(first, last, one, 0, unroll=True)


def send(src, dst, ssem, rsem, target):
    pltpu.make_async_remote_copy(
        src_ref=src, dst_ref=dst, send_sem=ssem, recv_sem=rsem, device_id=target, device_id_type=MESH
    ).start()


def await_bytes(ref, sem):
    pltpu.make_async_copy(ref, ref, sem).wait()


def iota(shape, dim):
    return lax.broadcasted_iota(jnp.int32, shape, dim)


def next_lat(v):
    return pltpu.roll(v, NLAT - 1, v.ndim - 1)


def last_lat(v):
    return pltpu.roll(v, 1, v.ndim - 1)


def next_row(v):
    return pltpu.roll(v, 15, 0)


def last_row(v):
    return pltpu.roll(v, 1, 0)


def blocks_to_lanes(blocks):
    lane = iota((8, 128), 1)
    tiles = []
    for t in range(6):
        b = (128 * t) // 96
        first, second = 96 * b - 128 * t, 96 * (b + 1) - 128 * t
        low = pltpu.roll(blocks[b], first % 128, 1) if first % 128 else blocks[b]
        high = pltpu.roll(blocks[b + 1], second % 128, 1)
        tiles.append(jnp.where(lane < second, low, high))
    return tiles


def lanes_to_blocks(tiles):
    lane = iota((8, 128), 1)
    blocks = []
    for b in range(8):
        t, offset = (96 * b) // 128, (96 * b) % 128
        block = pltpu.roll(tiles[t], 128 - offset, 1) if offset else tiles[t]
        if offset > 32:
            block = jnp.where(lane < 128 - offset, block, pltpu.roll(tiles[t + 1], 128 - offset, 1))
        blocks.append(jnp.where(lane < 96, block, 0.0))
    return blocks


def split(v):
    high = v.astype(jnp.bfloat16)
    return high, (v - high.astype(jnp.float32)).astype(jnp.bfloat16)


def kernel(
    lv_hbm, u_hbm, ice_hbm, steps_ref, cells_hbm, observed_hbm, weight_hbm,
    grad_ref, misfit_ref,
    lv_ref, u_ref, ice_ref, cells_ref, observed_ref, weight_ref,
    X, E, S1, QA, QO, QR, radS, radR, lonS, lonR,
    packet, gathered, block, sites, SB, RB, KH, KL,
    PB, C1R, C2S, C2R, C3S, C3R, SD, DR, ssem, rsem, isem,
):
    lon, rad = lax.axis_index("lon"), lax.axis_index("rad")
    y, z, c, x = place()
    own_block = y * 2 + c
    right, left = ((lon + 1) % 64, rad), ((lon + 63) % 64, rad)
    above, below = (lon, lax.min(rad + 1, 7)), (lon, lax.max(rad - 1, 0))

    barrier = pltpu.get_barrier_semaphore()

    def greet(target):
        pl.semaphore_signal(barrier, 1, device_id=target, device_id_type=MESH)

    has_above, has_below = rad < 7, rad > 0
    pl.when(has_above)(lambda: greet(above))
    pl.when(has_below)(lambda: greet(below))
    greet(right)
    greet(left)
    repeat(1, 16, lambda i: greet(z_peer(i)[0]))
    repeat(1, 32, lambda i: greet(plane_peer(i)[0]))
    loads = [
        pltpu.make_async_copy(source, target, isem.at[k])
        for k, (source, target) in enumerate((
            (cells_hbm, cells_ref), (observed_hbm, observed_ref), (weight_hbm, weight_ref),
            (lv_hbm, lv_ref), (u_hbm, u_ref), (ice_hbm, ice_ref),
        ))
    ]
    for load in loads:
        load.start()
    for load in loads:
        load.wait()

    for f in range(4):
        for l in range(COLS):
            source = lv_ref[:, l, :] if f == 0 else u_ref[f - 1, :, l, :]
            X[f, l + 2, 0:ROWS, :] = source
            X[f, l + 2, ROWS:16, :] = jnp.zeros((16 - ROWS, NLAT), jnp.float32)
            radS[0, f * 4 + l : f * 4 + l + 1, :] = source[11:12, :]
            radS[1, f * 4 + l : f * 4 + l + 1, :] = source[0:1, :]
            if l == COLS - 1:
                lonS[0, f * ROWS : f * ROWS + ROWS, :] = source
            if l == 0:
                lonS[1, f * ROWS : f * ROWS + ROWS, :] = source
    packet[...] = jnp.zeros((8, 128), jnp.float32)
    packet[0:1, 0:12] = cells_ref[...].astype(jnp.float32)
    packet[1:4, 0:12] = observed_ref[...]
    packet[4:7, 0:12] = weight_ref[...]
    gathered[z % 8] = packet[...]
    nothing = jnp.zeros((16, NLAT), jnp.float32)

    @pl.when(rad == 7)
    def no_layer_above():
        radR[1] = nothing
        radR[3] = nothing

    @pl.when(rad == 0)
    def no_layer_below():
        radR[0] = nothing
        radR[2] = nothing

    pl.semaphore_wait(barrier, 48 + lax.min(rad, 1) + lax.min(7 - rad, 1))

    pl.when(has_above)(lambda: send(radS.at[0], radR.at[0], ssem.at[0], rsem.at[0], above))
    pl.when(has_below)(lambda: send(radS.at[1], radR.at[1], ssem.at[1], rsem.at[1], below))

    def send_record(i):
        target, unused = z_peer((i + 12) % 16)
        send(packet, gathered.at[z % 8], ssem.at[4], rsem.at[4], target)

    repeat(0, 4, send_record)
    repeat(5, 8, send_record)
    send(lonS.at[0, pl.ds(0, 48)], lonR.at[0, pl.ds(0, 48)], ssem.at[2], rsem.at[2], right)
    send(lonS.at[1, pl.ds(0, 48)], lonR.at[1, pl.ds(0, 48)], ssem.at[3], rsem.at[3], left)

    row = iota((16, NLAT), 0)
    layer = jnp.where(row >= 14, row - 16, row)
    depth = (layer + rad * ROWS).astype(jnp.float32)
    wr = jnp.exp(4.0 * (depth - (NR - 1)) / NR)
    wr_next = jnp.exp(4.0 * (depth + 1.0 - (NR - 1)) / NR)
    own_row = row < ROWS
    wr_own = jnp.where(own_row, wr, 0.0)
    deep = layer + rad * ROWS
    face_ok = (row != 13) & (deep >= 0) & (deep < NR - 1)
    not_last = iota((16, NLAT), 1) < NLAT - 1
    is_top = jnp.where(rad == 7, 1.0, 0.0)

    await_bytes(gathered.at[pl.ds(0, 7)], rsem.at[4])
    record = gathered[0]
    for slot in range(1, 8):
        record = record + pltpu.roll(gathered[slot], 12 * slot, 1)
    block[...] = record
    sites[own_block] = record

    def send_block(i):
        target, unused = block_peer(i)
        send(block, sites.at[own_block], ssem.at[5], rsem.at[5], target)

    repeat(1, 8, send_block)

    await_bytes(lonR.at[0, pl.ds(0, 48)], rsem.at[2])
    await_bytes(lonR.at[1, pl.ds(0, 48)], rsem.at[3])
    for f in range(4):
        for side, p in ((0, 1), (1, 6)):
            X[f, p, 0:ROWS, :] = lonR[side, f * ROWS : f * ROWS + ROWS, :]
            X[f, p, ROWS:16, :] = jnp.zeros((16 - ROWS, NLAT), jnp.float32)
    pl.when(has_below)(lambda: await_bytes(radR.at[0], rsem.at[0]))
    pl.when(has_above)(lambda: await_bytes(radR.at[1], rsem.at[1]))
    for f in range(4):
        for l in range(COLS):
            X[f, l + 2, 15:16, :] = radR[0, f * 4 + l : f * 4 + l + 1, :]
            X[f, l + 2, 12:13, :] = radR[1, f * 4 + l : f * 4 + l + 1, :]

    def edge_lat(e):
        return jnp.where(not_last, 0.1 / (e + next_lat(e)), 0.0)

    def edge_rad(e):
        return jnp.where(face_ok, 0.1 / (e + next_row(e)), 0.0)

    for p in range(1, 7):
        E[p] = jnp.exp(X[0, p])
    for p in range(2, 6):
        QA[p] = edge_lat(E[p])
        QR[p] = edge_rad(E[p])
    for p in range(1, 6):
        QO[p] = 0.1 / (E[p] + E[p + 1])
    load_1, load_2 = ice_ref[steps_ref[0]], ice_ref[steps_ref[1]]
    for f in range(3):
        for p in range(2, 6):
            u = X[f + 1, p]
            flux = QA[p] * (next_lat(u) - u)
            rise = QR[p] * (next_row(u) - u)
            total = u + (flux - last_lat(flux)) + (rise - last_row(rise))
            total = total + QO[p] * (X[f + 1, p + 1] - u) + QO[p - 1] * (X[f + 1, p - 1] - u)
            if f == 0:
                pressed = jnp.broadcast_to(load_1[p - 2 : p - 1, :], (16, NLAT)) * is_top
                total = total - jnp.where(row == ROWS - 1, pressed, 0.0)
            S1[f, p] = total

    columns = []
    for f in range(3):
        columns.append([jnp.zeros((1, NLAT), jnp.float32) for unused in range(8)])

    def column_sum(v):
        return jnp.sum(v, axis=0, keepdims=True)

    for p in range(2, 6):
        slope = QR[p] * (wr_next - wr)
        factor = jnp.where(own_row, wr + slope - last_row(slope), 0.0)
        along = wr_own * QA[p]
        for f in range(3):
            s = S1[f, p]
            flux = column_sum(along * (next_lat(s) - s))
            columns[f][p] = columns[f][p] + column_sum(factor * s) + (flux - last_lat(flux))
    for p in range(1, 6):
        across = wr_own * QO[p]
        for f in range(3):
            if p == 1:
                flow = column_sum(across * S1[f, 2])
            elif p == 5:
                flow = -column_sum(across * S1[f, 5])
            else:
                flow = column_sum(across * (S1[f, p + 1] - S1[f, p]))
            columns[f][p] = columns[f][p] + flow
            columns[f][p + 1] = columns[f][p + 1] - flow
    for p in range(2, 6):
        columns[0][p] = columns[0][p] - load_2[p - 2 : p - 1, :] * is_top
    for f in range(3):
        for p in range(8):
            for band in range(4):
                SB[band, f * 8 + p : f * 8 + p + 1, :] = columns[f][p][:, band * 128 : band * 128 + 128]
    RB[x] = SB[x]

    def send_band(i):
        target, x2 = x_peer(i)
        send(SB.at[x2], RB.at[x], ssem.at[6], rsem.at[6], target)

    repeat(1, 4, send_band)

    for f in range(3):
        for l in range(COLS):
            radS[2, f * 4 + l : f * 4 + l + 1, :] = S1[f, l + 2, 11:12, :]
            radS[3, f * 4 + l : f * 4 + l + 1, :] = S1[f, l + 2, 0:1, :]
    for l in range(COLS):
        radS[2, 12 + l : 13 + l, :] = X[0, l + 2, 10:11, :]
        radS[3, 12 + l : 13 + l, :] = X[0, l + 2, 1:2, :]
    for side, edge, inner in ((2, 5, 4), (3, 2, 3)):
        for f in range(3):
            lonS[side, f * ROWS : f * ROWS + ROWS, :] = S1[f, edge, 0:ROWS, :]
        lonS[side, 36:48, :] = X[0, inner, 0:ROWS, :]
        lonS[side, 48:52, :] = X[0, edge, ROWS:16, :]
        lonS[side, 52:56, :] = jnp.zeros((4, NLAT), jnp.float32)
    pl.when(has_above)(lambda: send(radS.at[2], radR.at[2], ssem.at[7], rsem.at[7], above))
    pl.when(has_below)(lambda: send(radS.at[3], radR.at[3], ssem.at[8], rsem.at[8], below))
    send(lonS.at[2], lonR.at[2], ssem.at[9], rsem.at[9], right)
    send(lonS.at[3], lonR.at[3], ssem.at[10], rsem.at[10], left)

    await_bytes(sites.at[pl.ds(0, 7)], rsem.at[5])
    tiles = blocks_to_lanes([sites[b] for b in range(8)])
    theta = (iota((128, 128), 0) + x * 128).astype(jnp.float32)
    theta = math.pi * (theta + 0.5) / NLAT
    cell_cos, cell_sin = jnp.cos(theta), jnp.sin(theta)
    plane_lon = (iota((8, 128), 0) + (lon * COLS - 2)).astype(jnp.float32)
    for t in range(6):
        cell = jnp.broadcast_to(tiles[t][0:1, :], (8, 128))
        site_lon = jnp.floor(cell * (1.0 / NLAT))
        site_theta = math.pi * (cell - NLAT * site_lon + 0.5) / NLAT
        up = jnp.cos(site_theta)
        side = jnp.sin(site_theta) * jnp.cos(2.0 * math.pi * (site_lon - plane_lon) / NLON)
        for p in range(8):
            cosine = cell_cos * up[0:1, :] + cell_sin * side[p : p + 1, :]
            chord = 2.0 - 2.0 * cosine
            turns = chord * (40.0 / (2.0 * math.pi))
            turns = 0.25 - jnp.abs(turns - jnp.round(turns))
            squared = turns * turns
            wave = jnp.full_like(squared, WAVE[5])
            for k in range(4, -1, -1):
                wave = wave * squared + WAVE[k]
            value = 1.0 / (1.0 + chord * 10.0) + wave * turns
            high, low = split(value)
            KH[p * 128 : p * 128 + 128, t * 128 : t * 128 + 128] = high
            KL[p * 128 : p * 128 + 128, t * 128 : t * 128 + 128] = low

    await_bytes(RB.at[pl.ds(0, 3)], rsem.at[6])
    band = (RB[0] + RB[1]) + (RB[2] + RB[3])
    place_of = iota((24, 128), 0) % 8
    wide = jnp.concatenate([jnp.where(place_of == p, band, 0.0) for p in range(8)], axis=1)
    high, low = split(wide)
    dot = functools.partial(jnp.dot, preferred_element_type=jnp.float32)
    parts = dot(high, KH[...]) + dot(high, KL[...]) + dot(low, KH[...])
    row8 = iota((8, 6 * 128), 0)
    pred = jnp.zeros((8, 6 * 128), jnp.float32)
    for f in range(3):
        summed = jnp.sum(parts[f * 8 : f * 8 + 8, :], axis=0, keepdims=True) * SCALE
        pred = jnp.where(row8 == f, jnp.broadcast_to(summed, pred.shape), pred)
    pieces = lanes_to_blocks([pred[:, t * 128 : t * 128 + 128] for t in range(6)])
    for b in range(8):
        PB[b] = pieces[b][0:3]
    C1R[x * 8 + own_block] = PB[own_block]

    def send_piece(i):
        target, unused, b2 = plane_peer(i)
        send(PB.at[b2], C1R.at[x * 8 + own_block], ssem.at[13], rsem.at[13], target)

    repeat(1, 32, send_piece)
    await_bytes(C1R.at[pl.ds(0, 31)], rsem.at[13])
    summed = jnp.sum(C1R[...], axis=0)
    C2S[...] = summed
    C2R[z] = summed

    def send_sum(i):
        target, unused = z_peer(i)
        send(C2S, C2R.at[z], ssem.at[14], rsem.at[14], target)

    repeat(1, 16, send_sum)

    pl.when(has_below)(lambda: await_bytes(radR.at[2], rsem.at[7]))
    pl.when(has_above)(lambda: await_bytes(radR.at[3], rsem.at[8]))
    await_bytes(lonR.at[2], rsem.at[9])
    await_bytes(lonR.at[3], rsem.at[10])
    for f in range(3):
        for l in range(COLS):
            S1[f, l + 2, 15:16, :] = radR[2, f * 4 + l : f * 4 + l + 1, :]
            S1[f, l + 2, 12:13, :] = radR[3, f * 4 + l : f * 4 + l + 1, :]
    for l in range(COLS):
        X[0, l + 2, 14:15, :] = radR[2, 12 + l : 13 + l, :]
        X[0, l + 2, 13:14, :] = radR[3, 12 + l : 13 + l, :]
    for side, far, near in ((2, 0, 1), (3, 7, 6)):
        for f in range(3):
            S1[f, near, 0:ROWS, :] = lonR[side, f * ROWS : f * ROWS + ROWS, :]
            S1[f, near, ROWS:16, :] = jnp.zeros((16 - ROWS, NLAT), jnp.float32)
        X[0, far, 0:ROWS, :] = lonR[side, 36:48, :]
        X[0, far, ROWS:16, :] = jnp.zeros((16 - ROWS, NLAT), jnp.float32)
        X[0, near, ROWS:16, :] = lonR[side, 48:52, :]
    for p in range(8):
        E[p] = jnp.exp(X[0, p])
    for p in range(1, 7):
        QA[p] = edge_lat(E[p])
        QR[p] = edge_rad(E[p])
    for p in range(7):
        QO[p] = 0.1 / (E[p] + E[p + 1])

    await_bytes(C2R.at[pl.ds(0, 15)], rsem.at[14])
    predicted = jnp.concatenate([jnp.sum(C2R[...], axis=0), jnp.zeros((5, 128), jnp.float32)], axis=0)
    record = block[...]
    row_of, lane_of = iota((8, 128), 0), iota((8, 128), 1)
    entry = (row_of < 3) & (lane_of < 96)
    weight = jnp.where(entry, pltpu.roll(record, 4, 0), 0.0)
    weighted = weight * (predicted - pltpu.roll(record, 7, 0))
    squares = jnp.broadcast_to(jnp.sum(weighted * weighted, axis=0, keepdims=True), (8, 128))
    pulled = jnp.where(row_of == 3, squares, weight * weighted)
    C3S[...] = pulled[0:4]
    C3R[own_block] = pulled[0:4]

    def send_pulled(i):
        target, unused = block_peer(i)
        send(C3S, C3R.at[own_block], ssem.at[15], rsem.at[15], target)

    repeat(1, 8, send_pulled)
    await_bytes(C3R.at[pl.ds(0, 7)], rsem.at[15])
    pulls = [jnp.concatenate([C3R[b], jnp.zeros((4, 128), jnp.float32)], axis=0) for b in range(8)]
    total = pulls[0]
    for b in range(1, 8):
        total = total + pulls[b]
    misfit_ref[0] = jnp.sum(total[3:4, :]) / (3.0 * 768.0)
    pull = jnp.concatenate(blocks_to_lanes(pulls), axis=1)
    high, low = split(pull)
    both = jnp.concatenate([high, low], axis=0)

    def against(lhs, rhs):
        return lax.dot_general(lhs, rhs, (((1,), (1,)), ((), ())), preferred_element_type=jnp.float32)

    first = against(both, KH[...])
    adjoint = (first[0:8] + first[8:16] + against(both, KL[...])[0:8]) * SCALE
    SD[...] = adjoint[0:3]
    DR[x] = adjoint[0:3]

    def send_adjoint(i):
        target, unused = x_peer(i)
        send(SD, DR.at[x], ssem.at[16], rsem.at[16], target)

    repeat(1, 4, send_adjoint)
    await_bytes(DR.at[pl.ds(0, 3)], rsem.at[16])

    faces_a = [jnp.zeros((16, NLAT), jnp.float32) for unused in range(8)]
    faces_r = [jnp.zeros((16, NLAT), jnp.float32) for unused in range(8)]
    faces_o = [jnp.zeros((16, NLAT), jnp.float32) for unused in range(8)]
    for f in range(3):
        a2 = []
        for p in range(8):
            surface = jnp.concatenate(
                [DR[band, f : f + 1, p * 128 : p * 128 + 128] for band in range(4)], axis=1
            )
            a2.append(wr * jnp.broadcast_to(surface, (16, NLAT)))
        a1 = [None] * 8
        for p in range(1, 7):
            flux = QA[p] * (next_lat(a2[p]) - a2[p])
            rise = QR[p] * (next_row(a2[p]) - a2[p])
            a1[p] = (
                a2[p] + (flux - last_lat(flux)) + (rise - last_row(rise))
                + QO[p] * (a2[p + 1] - a2[p]) + QO[p - 1] * (a2[p - 1] - a2[p])
            )
        for p in range(1, 6):
            u, s = X[f + 1, p], S1[f, p]
            faces_o[p] = (
                faces_o[p]
                + (X[f + 1, p + 1] - u) * (a1[p + 1] - a1[p])
                + (S1[f, p + 1] - s) * (a2[p + 1] - a2[p])
            )
            if p > 1:
                faces_a[p] = (
                    faces_a[p]
                    + (next_lat(u) - u) * (next_lat(a1[p]) - a1[p])
                    + (next_lat(s) - s) * (next_lat(a2[p]) - a2[p])
                )
                faces_r[p] = (
                    faces_r[p]
                    + (next_row(u) - u) * (next_row(a1[p]) - a1[p])
                    + (next_row(s) - s) * (next_row(a2[p]) - a2[p])
                )
    for p in range(1, 6):
        faces_o[p] = QO[p] * QO[p] * faces_o[p]
    for p in range(2, 6):
        along = QA[p] * QA[p] * faces_a[p]
        upward = QR[p] * QR[p] * faces_r[p]
        whole = (along + last_lat(along)) + (upward + last_row(upward)) + (faces_o[p] + faces_o[p - 1])
        result = 10.0 * E[p] * whole + 0.1 * X[0, p]
        grad_ref[:, p - 2, :] = result[0:ROWS, :]

    pl.when(has_above)(lambda: await_bytes(radS.at[0], ssem.at[0]))
    pl.when(has_below)(lambda: await_bytes(radS.at[1], ssem.at[1]))
    pl.when(has_above)(lambda: await_bytes(radS.at[2], ssem.at[7]))
    pl.when(has_below)(lambda: await_bytes(radS.at[3], ssem.at[8]))
    for k, ref in ((2, lonS.at[0, pl.ds(0, 48)]), (3, lonS.at[1, pl.ds(0, 48)]), (4, gathered.at[pl.ds(0, 7)]),
                   (5, sites.at[pl.ds(0, 7)]), (6, RB.at[pl.ds(0, 3)]), (9, lonS.at[2]), (10, lonS.at[3]),
                   (13, C1R.at[pl.ds(0, 31)]), (14, C2R.at[pl.ds(0, 15)]),
                   (15, C3R.at[pl.ds(0, 7)]), (16, DR.at[pl.ds(0, 3)])):
        await_bytes(ref, ssem.at[k])


def body(logvisc, momentum, displacement, ice_history, load_steps, site_cells, observed, site_weight):
    f32 = jnp.float32
    vmem = pl.BlockSpec(memory_space=pltpu.VMEM)
    smem = pl.BlockSpec(memory_space=pltpu.SMEM)
    hbm = pl.BlockSpec(memory_space=pltpu.HBM)
    gradient, misfit = pl.pallas_call(
        kernel,
        out_shape=(
            jax.ShapeDtypeStruct((ROWS, COLS, NLAT), f32),
            jax.ShapeDtypeStruct((1,), f32),
        ),
        in_specs=[hbm, hbm, hbm, smem, hbm, hbm, hbm],
        out_specs=(vmem, smem),
        scratch_shapes=[
            pltpu.VMEM((ROWS, COLS, NLAT), f32),
            pltpu.VMEM((3, ROWS, COLS, NLAT), f32),
            pltpu.VMEM((8, COLS, NLAT), f32),
            pltpu.VMEM((1, 12), jnp.int32),
            pltpu.VMEM((3, 12), f32),
            pltpu.VMEM((3, 12), f32),
            pltpu.VMEM((4, 8, 16, NLAT), f32),
            pltpu.VMEM((8, 16, NLAT), f32),
            pltpu.VMEM((3, 8, 16, NLAT), f32),
            pltpu.VMEM((8, 16, NLAT), f32),
            pltpu.VMEM((8, 16, NLAT), f32),
            pltpu.VMEM((8, 16, NLAT), f32),
            pltpu.VMEM((4, 16, NLAT), f32),
            pltpu.VMEM((4, 16, NLAT), f32),
            pltpu.VMEM((4, 56, NLAT), f32),
            pltpu.VMEM((4, 56, NLAT), f32),
            pltpu.VMEM((8, 128), f32),
            pltpu.VMEM((8, 8, 128), f32),
            pltpu.VMEM((8, 128), f32),
            pltpu.VMEM((8, 8, 128), f32),
            pltpu.VMEM((4, 24, 128), f32),
            pltpu.VMEM((4, 24, 128), f32),
            pltpu.VMEM((1024, 768), jnp.bfloat16),
            pltpu.VMEM((1024, 768), jnp.bfloat16),
            pltpu.VMEM((8, 3, 128), f32),
            pltpu.VMEM((32, 3, 128), f32),
            pltpu.VMEM((3, 128), f32),
            pltpu.VMEM((16, 3, 128), f32),
            pltpu.VMEM((4, 128), f32),
            pltpu.VMEM((8, 4, 128), f32),
            pltpu.VMEM((3, 1024), f32),
            pltpu.VMEM((4, 3, 1024), f32),
            pltpu.SemaphoreType.DMA((17,)),
            pltpu.SemaphoreType.DMA((17,)),
            pltpu.SemaphoreType.DMA((6,)),
        ],
        compiler_params=pltpu.CompilerParams(
            collective_id=0, has_side_effects=True, vmem_limit_bytes=62 * 1024 * 1024
        ),
    )(logvisc, displacement, ice_history, load_steps, site_cells.reshape(1, 12), observed, site_weight)
    half_momentum = momentum - 0.5 * gradient
    return logvisc + half_momentum, half_momentum, misfit


def solution(mesh):
    return jax.shard_map(
        body,
        mesh=mesh,
        in_specs=(
            P("rad", "lon", None),
            P("rad", "lon", None),
            P(None, "rad", "lon", None),
            P(None, "lon", None),
            P(),
            P("lon"),
            P(None, "lon"),
            P(None, "lon"),
        ),
        out_specs=(P("rad", "lon", None), P("rad", "lon", None), P()),
        check_vma=False,
    )
```

```python
import functools
import math

import jax
import jax.numpy as jnp
from jax import lax
from jax.experimental import pallas as pl
from jax.experimental.pallas import tpu as pltpu
from jax.sharding import PartitionSpec as P

MESH = pl.DeviceIdType.MESH
NR, NLON, NLAT = 96, 256, 512
ROWS = 12
COLS = 4
SCALE = 1.0 / math.sqrt(NLON * NLAT)
WAVE = [0.5 * (-1) ** k * (2.0 * math.pi) ** (2 * k + 1) / math.factorial(2 * k + 1) for k in range(6)]


def place():
    lon, rad = lax.axis_index("lon"), lax.axis_index("rad")
    return lon // 16, (rad // 4) * 8 + (lon // 2) % 8, lon % 2, rad % 4


def device(y, z, c, x):
    return (y * 16 + (z % 8) * 2 + c, (z // 8) * 4 + x)


def z_peer(i):
    y, z, c, x = place()
    z2 = (z + i) % 16
    return device(y, z2, c, x), z2


def plane_peer(i):
    y, z, c, x = place()
    x2, y2, c2 = (x + i % 4) % 4, (y + (i // 4) % 4) % 4, (c + i // 16) % 2
    return device(y2, z, c2, x2), x2, y2 * 2 + c2


def block_peer(i):
    y, z, c, x = place()
    y2, c2 = (y + i % 4) % 4, (c + i // 4) % 2
    return device(y2, z, c2, x), y2 * 2 + c2


def x_peer(i):
    y, z, c, x = place()
    x2 = (x + i) % 4
    return device(y, z, c, x2), x2


def repeat(first, last, step):
    for i in range(first, last):
        step(i)


def ring(offset, size):
    return min(offset % size, size - offset % size)


FAR_Z = sorted(range(1, 16), key=lambda i: -ring(i, 16))
FAR_PLANE = sorted(range(1, 32), key=lambda i: -(ring(i, 4) + ring(i // 4, 4) + 0.5 * (i // 16)))


def send(src, dst, ssem, rsem, target):
    pltpu.make_async_remote_copy(
        src_ref=src, dst_ref=dst, send_sem=ssem, recv_sem=rsem, device_id=target, device_id_type=MESH
    ).start()


def await_bytes(ref, sem):
    pltpu.make_async_copy(ref, ref, sem).wait()


def iota(shape, dim):
    return lax.broadcasted_iota(jnp.int32, shape, dim)


def next_lat(v):
    return pltpu.roll(v, NLAT - 1, v.ndim - 1)


def last_lat(v):
    return pltpu.roll(v, 1, v.ndim - 1)


def next_row(v):
    return pltpu.roll(v, 15, 0)


def last_row(v):
    return pltpu.roll(v, 1, 0)


def blocks_to_lanes(blocks):
    lane = iota((8, 128), 1)
    tiles = []
    for t in range(6):
        b = (128 * t) // 96
        first, second = 96 * b - 128 * t, 96 * (b + 1) - 128 * t
        low = pltpu.roll(blocks[b], first % 128, 1) if first % 128 else blocks[b]
        high = pltpu.roll(blocks[b + 1], second % 128, 1)
        tiles.append(jnp.where(lane < second, low, high))
    return tiles


def lanes_to_blocks(tiles):
    lane = iota((8, 128), 1)
    blocks = []
    for b in range(8):
        t, offset = (96 * b) // 128, (96 * b) % 128
        block = pltpu.roll(tiles[t], 128 - offset, 1) if offset else tiles[t]
        if offset > 32:
            block = jnp.where(lane < 128 - offset, block, pltpu.roll(tiles[t + 1], 128 - offset, 1))
        blocks.append(jnp.where(lane < 96, block, 0.0))
    return blocks


def split(v):
    high = v.astype(jnp.bfloat16)
    return high, (v - high.astype(jnp.float32)).astype(jnp.bfloat16)


def kernel(
    lv_hbm, u_hbm, ice_hbm, steps_ref, cells_hbm, observed_hbm, weight_hbm,
    grad_ref, misfit_ref,
    lv_ref, u_ref, ice_ref, cells_ref, observed_ref, weight_ref,
    X, E, S1, QA, QO, QR, radS, radR, lonS, lonR,
    packet, gathered, block, sites, SB, RB, KH, KL,
    PB, C1R, C2S, C2R, C3S, C3R, SD, DR,
    TH, TL, AS, AA, AL, AO, UO, SO, UA, SA, UR, SR, ssem, rsem, isem,
):
    lon, rad = lax.axis_index("lon"), lax.axis_index("rad")
    y, z, c, x = place()
    own_block = y * 2 + c
    right, left = ((lon + 1) % 64, rad), ((lon + 63) % 64, rad)
    above, below = (lon, lax.min(rad + 1, 7)), (lon, lax.max(rad - 1, 0))

    barrier = pltpu.get_barrier_semaphore()

    def greet(target):
        pl.semaphore_signal(barrier, 1, device_id=target, device_id_type=MESH)

    has_above, has_below = rad < 7, rad > 0
    pl.when(has_above)(lambda: greet(above))
    pl.when(has_below)(lambda: greet(below))
    greet(right)
    greet(left)
    for i in FAR_Z:
        greet(z_peer(i)[0])
    for i in FAR_PLANE:
        greet(plane_peer(i)[0])
    loads = [
        pltpu.make_async_copy(source, target, isem.at[k])
        for k, (source, target) in enumerate((
            (cells_hbm, cells_ref), (observed_hbm, observed_ref), (weight_hbm, weight_ref),
            (lv_hbm, lv_ref), (u_hbm, u_ref), (ice_hbm, ice_ref),
        ))
    ]
    for load in loads:
        load.start()
    for load in loads:
        load.wait()

    for f in range(4):
        for l in range(COLS):
            source = lv_ref[:, l, :] if f == 0 else u_ref[f - 1, :, l, :]
            X[f, l + 2, 0:ROWS, :] = source
            X[f, l + 2, ROWS:16, :] = jnp.zeros((16 - ROWS, NLAT), jnp.float32)
            radS[0, f * 4 + l : f * 4 + l + 1, :] = source[11:12, :]
            radS[1, f * 4 + l : f * 4 + l + 1, :] = source[0:1, :]
            if l == COLS - 1:
                lonS[0, f * ROWS : f * ROWS + ROWS, :] = source
            if l == 0:
                lonS[1, f * ROWS : f * ROWS + ROWS, :] = source
    packet[...] = jnp.zeros((8, 128), jnp.float32)
    packet[0:1, 0:12] = cells_ref[...].astype(jnp.float32)
    packet[1:4, 0:12] = observed_ref[...]
    packet[4:7, 0:12] = weight_ref[...]
    gathered[z % 8] = packet[...]
    nothing = jnp.zeros((16, NLAT), jnp.float32)

    @pl.when(rad == 7)
    def no_layer_above():
        radR[1] = nothing
        radR[3] = nothing

    @pl.when(rad == 0)
    def no_layer_below():
        radR[0] = nothing
        radR[2] = nothing

    pl.semaphore_wait(barrier, 48 + lax.min(rad, 1) + lax.min(7 - rad, 1))

    pl.when(has_above)(lambda: send(radS.at[0], radR.at[0], ssem.at[0], rsem.at[0], above))
    pl.when(has_below)(lambda: send(radS.at[1], radR.at[1], ssem.at[1], rsem.at[1], below))

    def send_record(i):
        target, unused = z_peer((i + 12) % 16)
        send(packet, gathered.at[z % 8], ssem.at[4], rsem.at[4], target)

    repeat(0, 4, send_record)
    repeat(5, 8, send_record)
    send(lonS.at[0, pl.ds(0, 48)], lonR.at[0, pl.ds(0, 48)], ssem.at[2], rsem.at[2], right)
    send(lonS.at[1, pl.ds(0, 48)], lonR.at[1, pl.ds(0, 48)], ssem.at[3], rsem.at[3], left)

    row = iota((16, NLAT), 0)
    layer = jnp.where(row >= 14, row - 16, row)
    depth = (layer + rad * ROWS).astype(jnp.float32)
    wr = jnp.exp(4.0 * (depth - (NR - 1)) / NR)
    wr_next = jnp.exp(4.0 * (depth + 1.0 - (NR - 1)) / NR)
    own_row = row < ROWS
    wr_own = jnp.where(own_row, wr, 0.0)
    deep = layer + rad * ROWS
    face_ok = (row != 13) & (deep >= 0) & (deep < NR - 1)
    not_last = iota((16, NLAT), 1) < NLAT - 1
    is_top = jnp.where(rad == 7, 1.0, 0.0)

    await_bytes(gathered.at[pl.ds(0, 7)], rsem.at[4])
    record = gathered[0]
    for slot in range(1, 8):
        record = record + pltpu.roll(gathered[slot], 12 * slot, 1)
    block[...] = record
    sites[own_block] = record

    def send_block(i):
        target, unused = block_peer(i)
        send(block, sites.at[own_block], ssem.at[5], rsem.at[5], target)

    repeat(1, 8, send_block)

    await_bytes(lonR.at[0, pl.ds(0, 48)], rsem.at[2])
    await_bytes(lonR.at[1, pl.ds(0, 48)], rsem.at[3])
    for f in range(4):
        for side, p in ((0, 1), (1, 6)):
            X[f, p, 0:ROWS, :] = lonR[side, f * ROWS : f * ROWS + ROWS, :]
            X[f, p, ROWS:16, :] = jnp.zeros((16 - ROWS, NLAT), jnp.float32)
    pl.when(has_below)(lambda: await_bytes(radR.at[0], rsem.at[0]))
    pl.when(has_above)(lambda: await_bytes(radR.at[1], rsem.at[1]))
    for f in range(4):
        for l in range(COLS):
            X[f, l + 2, 15:16, :] = radR[0, f * 4 + l : f * 4 + l + 1, :]
            X[f, l + 2, 12:13, :] = radR[1, f * 4 + l : f * 4 + l + 1, :]

    def edge_lat(e):
        return jnp.where(not_last, 0.1 / (e + next_lat(e)), 0.0)

    def edge_rad(e):
        return jnp.where(face_ok, 0.1 / (e + next_row(e)), 0.0)

    for p in range(1, 7):
        E[p] = jnp.exp(X[0, p])
    for p in range(2, 6):
        QA[p] = edge_lat(E[p])
        QR[p] = edge_rad(E[p])
    for p in range(1, 6):
        QO[p] = 0.1 / (E[p] + E[p + 1])
    load_1, load_2 = ice_ref[steps_ref[0]], ice_ref[steps_ref[1]]
    for f in range(3):
        for p in range(2, 6):
            u = X[f + 1, p]
            flux = QA[p] * (next_lat(u) - u)
            rise = QR[p] * (next_row(u) - u)
            total = u + (flux - last_lat(flux)) + (rise - last_row(rise))
            total = total + QO[p] * (X[f + 1, p + 1] - u) + QO[p - 1] * (X[f + 1, p - 1] - u)
            if f == 0:
                pressed = jnp.broadcast_to(load_1[p - 2 : p - 1, :], (16, NLAT)) * is_top
                total = total - jnp.where(row == ROWS - 1, pressed, 0.0)
            S1[f, p] = total

    columns = []
    for f in range(3):
        columns.append([jnp.zeros((1, NLAT), jnp.float32) for unused in range(8)])

    def column_sum(v):
        return jnp.sum(v, axis=0, keepdims=True)

    for p in range(2, 6):
        slope = QR[p] * (wr_next - wr)
        factor = jnp.where(own_row, wr + slope - last_row(slope), 0.0)
        along = wr_own * QA[p]
        for f in range(3):
            s = S1[f, p]
            flux = column_sum(along * (next_lat(s) - s))
            columns[f][p] = columns[f][p] + column_sum(factor * s) + (flux - last_lat(flux))
    for p in range(1, 6):
        across = wr_own * QO[p]
        for f in range(3):
            if p == 1:
                flow = column_sum(across * S1[f, 2])
            elif p == 5:
                flow = -column_sum(across * S1[f, 5])
            else:
                flow = column_sum(across * (S1[f, p + 1] - S1[f, p]))
            columns[f][p] = columns[f][p] + flow
            columns[f][p + 1] = columns[f][p + 1] - flow
    for p in range(2, 6):
        columns[0][p] = columns[0][p] - load_2[p - 2 : p - 1, :] * is_top
    for f in range(3):
        for p in range(8):
            for band in range(4):
                SB[band, f * 8 + p : f * 8 + p + 1, :] = columns[f][p][:, band * 128 : band * 128 + 128]
    RB[x] = SB[x]

    def send_band(i):
        target, x2 = x_peer(i)
        send(SB.at[x2], RB.at[x], ssem.at[6], rsem.at[6], target)

    repeat(1, 4, send_band)

    for f in range(3):
        for l in range(COLS):
            radS[2, f * 4 + l : f * 4 + l + 1, :] = S1[f, l + 2, 11:12, :]
            radS[3, f * 4 + l : f * 4 + l + 1, :] = S1[f, l + 2, 0:1, :]
    for l in range(COLS):
        radS[2, 12 + l : 13 + l, :] = X[0, l + 2, 10:11, :]
        radS[3, 12 + l : 13 + l, :] = X[0, l + 2, 1:2, :]
    for side, edge, inner in ((2, 5, 4), (3, 2, 3)):
        for f in range(3):
            lonS[side, f * ROWS : f * ROWS + ROWS, :] = S1[f, edge, 0:ROWS, :]
        lonS[side, 36:48, :] = X[0, inner, 0:ROWS, :]
        lonS[side, 48:52, :] = X[0, edge, ROWS:16, :]
        lonS[side, 52:56, :] = jnp.zeros((4, NLAT), jnp.float32)
    pl.when(has_above)(lambda: send(radS.at[2], radR.at[2], ssem.at[7], rsem.at[7], above))
    pl.when(has_below)(lambda: send(radS.at[3], radR.at[3], ssem.at[8], rsem.at[8], below))
    send(lonS.at[2], lonR.at[2], ssem.at[9], rsem.at[9], right)
    send(lonS.at[3], lonR.at[3], ssem.at[10], rsem.at[10], left)

    await_bytes(sites.at[pl.ds(0, 7)], rsem.at[5])
    tiles = blocks_to_lanes([sites[b] for b in range(8)])
    theta = (iota((128, 128), 0) + x * 128).astype(jnp.float32)
    theta = math.pi * (theta + 0.5) / NLAT
    cell_cos, cell_sin = jnp.cos(theta), jnp.sin(theta)
    plane_lon = (iota((8, 128), 0) + (lon * COLS - 2)).astype(jnp.float32)
    for t in range(6):
        cell = jnp.broadcast_to(tiles[t][0:1, :], (8, 128))
        site_lon = jnp.floor(cell * (1.0 / NLAT))
        site_theta = math.pi * (cell - NLAT * site_lon + 0.5) / NLAT
        up = jnp.cos(site_theta)
        side = jnp.sin(site_theta) * jnp.cos(2.0 * math.pi * (site_lon - plane_lon) / NLON)
        for p in range(8):
            cosine = cell_cos * up[0:1, :] + cell_sin * side[p : p + 1, :]
            chord = 2.0 - 2.0 * cosine
            turns = chord * (40.0 / (2.0 * math.pi))
            turns = 0.25 - jnp.abs(turns - jnp.round(turns))
            squared = turns * turns
            wave = jnp.full_like(squared, WAVE[5])
            for k in range(4, -1, -1):
                wave = wave * squared + WAVE[k]
            value = 1.0 / (1.0 + chord * 10.0) + wave * turns
            high, low = split(value)
            KH[p * 128 : p * 128 + 128, t * 128 : t * 128 + 128] = high
            KL[p * 128 : p * 128 + 128, t * 128 : t * 128 + 128] = low

    await_bytes(RB.at[pl.ds(0, 3)], rsem.at[6])
    band = (RB[0] + RB[1]) + (RB[2] + RB[3])
    place_of = iota((24, 128), 0) % 8
    wide = jnp.concatenate([jnp.where(place_of == p, band, 0.0) for p in range(1, 7)], axis=1)
    high, low = split(wide)
    dot = functools.partial(jnp.dot, preferred_element_type=jnp.float32)
    both = jnp.concatenate([high.astype(jnp.float32), low.astype(jnp.float32)], axis=0).astype(jnp.bfloat16)
    parts = dot(both, KH[128:896])
    parts = parts[0:24] + parts[24:48] + dot(high, KL[128:896])
    row8 = iota((8, 6 * 128), 0)
    pred = jnp.zeros((8, 6 * 128), jnp.float32)
    for f in range(3):
        summed = jnp.sum(parts[f * 8 : f * 8 + 8, :], axis=0, keepdims=True) * SCALE
        pred = jnp.where(row8 == f, jnp.broadcast_to(summed, pred.shape), pred)
    pieces = lanes_to_blocks([pred[:, t * 128 : t * 128 + 128] for t in range(6)])
    for b in range(8):
        PB[b] = pieces[b][0:3]
    C1R[x * 8 + own_block] = PB[own_block]

    def send_piece(i):
        target, unused, b2 = plane_peer(i)
        send(PB.at[b2], C1R.at[x * 8 + own_block], ssem.at[13], rsem.at[13], target)

    for i in FAR_PLANE:
        send_piece(i)
    await_bytes(C1R.at[pl.ds(0, 31)], rsem.at[13])
    summed = jnp.sum(C1R[...], axis=0)
    C2S[...] = summed
    C2R[z] = summed

    def send_sum(i):
        target, unused = z_peer(i)
        send(C2S, C2R.at[z], ssem.at[14], rsem.at[14], target)

    for i in FAR_Z:
        send_sum(i)

    pl.when(has_below)(lambda: await_bytes(radR.at[2], rsem.at[7]))
    pl.when(has_above)(lambda: await_bytes(radR.at[3], rsem.at[8]))
    await_bytes(lonR.at[2], rsem.at[9])
    await_bytes(lonR.at[3], rsem.at[10])
    for f in range(3):
        for l in range(COLS):
            S1[f, l + 2, 15:16, :] = radR[2, f * 4 + l : f * 4 + l + 1, :]
            S1[f, l + 2, 12:13, :] = radR[3, f * 4 + l : f * 4 + l + 1, :]
    for l in range(COLS):
        X[0, l + 2, 14:15, :] = radR[2, 12 + l : 13 + l, :]
        X[0, l + 2, 13:14, :] = radR[3, 12 + l : 13 + l, :]
    for side, far, near in ((2, 0, 1), (3, 7, 6)):
        for f in range(3):
            S1[f, near, 0:ROWS, :] = lonR[side, f * ROWS : f * ROWS + ROWS, :]
            S1[f, near, ROWS:16, :] = jnp.zeros((16 - ROWS, NLAT), jnp.float32)
        X[0, far, 0:ROWS, :] = lonR[side, 36:48, :]
        X[0, far, ROWS:16, :] = jnp.zeros((16 - ROWS, NLAT), jnp.float32)
        X[0, near, ROWS:16, :] = lonR[side, 48:52, :]
    for p in range(8):
        E[p] = jnp.exp(X[0, p])
    for p in range(1, 7):
        QA[p] = edge_lat(E[p])
        QR[p] = edge_rad(E[p])
    for p in range(7):
        QO[p] = 0.1 / (E[p] + E[p + 1])
    for p in range(1, 7):
        slope = QR[p] * (wr_next - wr)
        AS[p] = wr + slope - last_row(slope)
        along = QA[p] * wr
        AA[p] = along
        AL[p] = last_lat(along)
    for p in range(7):
        AO[p] = QO[p] * wr
    for f in range(3):
        for p in range(1, 6):
            u, s, square = X[f + 1, p], S1[f, p], QO[p] * QO[p]
            UO[f, p] = square * (X[f + 1, p + 1] - u)
            SO[f, p] = square * wr * (S1[f, p + 1] - s)
            if p > 1:
                square = QA[p] * QA[p]
                UA[f, p] = square * (next_lat(u) - u)
                SA[f, p] = square * wr * (next_lat(s) - s)
                square = QR[p] * QR[p]
                UR[f, p] = square * (next_row(u) - u)
                SR[f, p] = square * (wr_next - wr) * (next_row(s) - s)
    for t in range(6):
        for p in range(8):
            TH[t * 128 : t * 128 + 128, p * 128 : p * 128 + 128] = KH[p * 128 : p * 128 + 128, t * 128 : t * 128 + 128].T
            TL[t * 128 : t * 128 + 128, p * 128 : p * 128 + 128] = KL[p * 128 : p * 128 + 128, t * 128 : t * 128 + 128].T

    await_bytes(C2R.at[pl.ds(0, 15)], rsem.at[14])
    predicted = jnp.concatenate([jnp.sum(C2R[...], axis=0), jnp.zeros((5, 128), jnp.float32)], axis=0)
    record = block[...]
    row_of, lane_of = iota((8, 128), 0), iota((8, 128), 1)
    entry = (row_of < 3) & (lane_of < 96)
    weight = jnp.where(entry, pltpu.roll(record, 4, 0), 0.0)
    weighted = weight * (predicted - pltpu.roll(record, 7, 0))
    squares = jnp.broadcast_to(jnp.sum(weighted * weighted, axis=0, keepdims=True), (8, 128))
    pulled = jnp.where(row_of == 3, squares, weight * weighted)
    C3S[...] = pulled[0:4]
    C3R[own_block] = pulled[0:4]

    def send_pulled(i):
        target, unused = block_peer(i)
        send(C3S, C3R.at[own_block], ssem.at[15], rsem.at[15], target)

    repeat(1, 8, send_pulled)
    await_bytes(C3R.at[pl.ds(0, 7)], rsem.at[15])
    pulls = [jnp.concatenate([C3R[b], jnp.zeros((4, 128), jnp.float32)], axis=0) for b in range(8)]
    total = pulls[0]
    for b in range(1, 8):
        total = total + pulls[b]
    misfit_ref[0] = jnp.sum(total[3:4, :]) / (3.0 * 768.0)
    pull = jnp.concatenate(blocks_to_lanes(pulls), axis=1)
    high, low = split(pull)
    both = jnp.concatenate([high, low], axis=0)

    first = dot(both, TH[...])
    adjoint = (first[0:8] + first[8:16] + dot(both, TL[...])[0:8]) * SCALE
    for f in range(3):
        for p in range(8):
            SD[f * 8 + p : f * 8 + p + 1, :] = adjoint[f : f + 1, p * 128 : p * 128 + 128]
    DR[x] = SD[...]

    def send_adjoint(i):
        target, unused = x_peer(i)
        send(SD, DR.at[x], ssem.at[16], rsem.at[16], target)

    repeat(1, 4, send_adjoint)
    await_bytes(DR.at[pl.ds(0, 3)], rsem.at[16])

    faces_a = [jnp.zeros((16, NLAT), jnp.float32) for unused in range(8)]
    faces_r = [jnp.zeros((16, NLAT), jnp.float32) for unused in range(8)]
    faces_o = [jnp.zeros((16, NLAT), jnp.float32) for unused in range(8)]

    def spread(v, p):
        return jnp.broadcast_to(v[p : p + 1, :], (16, NLAT))

    for f in range(3):
        surface = jnp.concatenate([DR[band, f * 8 : f * 8 + 8, :] for band in range(4)], axis=1)
        step = next_lat(surface) - surface
        step_before = last_lat(step)
        beside = [spread(surface, p + 1) - spread(surface, p) for p in range(7)]
        a1 = [None] * 8
        for p in range(1, 7):
            a1[p] = (
                AS[p] * spread(surface, p) + AA[p] * spread(step, p) - AL[p] * spread(step_before, p)
                + AO[p] * beside[p] - AO[p - 1] * beside[p - 1]
            )
        for p in range(1, 6):
            faces_o[p] = faces_o[p] + UO[f, p] * (a1[p + 1] - a1[p]) + SO[f, p] * beside[p]
            if p > 1:
                faces_a[p] = faces_a[p] + UA[f, p] * (next_lat(a1[p]) - a1[p]) + SA[f, p] * spread(step, p)
                faces_r[p] = faces_r[p] + UR[f, p] * (next_row(a1[p]) - a1[p]) + SR[f, p] * spread(surface, p)
    for p in range(2, 6):
        along, upward = faces_a[p], faces_r[p]
        whole = (along + last_lat(along)) + (upward + last_row(upward)) + (faces_o[p] + faces_o[p - 1])
        result = 10.0 * E[p] * whole + 0.1 * X[0, p]
        grad_ref[:, p - 2, :] = result[0:ROWS, :]

    pl.when(has_above)(lambda: await_bytes(radS.at[0], ssem.at[0]))
    pl.when(has_below)(lambda: await_bytes(radS.at[1], ssem.at[1]))
    pl.when(has_above)(lambda: await_bytes(radS.at[2], ssem.at[7]))
    pl.when(has_below)(lambda: await_bytes(radS.at[3], ssem.at[8]))
    for k, ref in ((2, lonS.at[0, pl.ds(0, 48)]), (3, lonS.at[1, pl.ds(0, 48)]), (4, gathered.at[pl.ds(0, 7)]),
                   (5, sites.at[pl.ds(0, 7)]), (6, RB.at[pl.ds(0, 3)]), (9, lonS.at[2]), (10, lonS.at[3]),
                   (13, C1R.at[pl.ds(0, 31)]), (14, C2R.at[pl.ds(0, 15)]),
                   (15, C3R.at[pl.ds(0, 7)]), (16, DR.at[pl.ds(0, 3)])):
        await_bytes(ref, ssem.at[k])


def body(logvisc, momentum, displacement, ice_history, load_steps, site_cells, observed, site_weight):
    f32 = jnp.float32
    vmem = pl.BlockSpec(memory_space=pltpu.VMEM)
    smem = pl.BlockSpec(memory_space=pltpu.SMEM)
    hbm = pl.BlockSpec(memory_space=pltpu.HBM)
    gradient, misfit = pl.pallas_call(
        kernel,
        out_shape=(
            pltpu.VMEM((ROWS, COLS, NLAT), f32),
            jax.ShapeDtypeStruct((1,), f32),
        ),
        in_specs=[hbm, hbm, hbm, smem, hbm, hbm, hbm],
        out_specs=(vmem, smem),
        scratch_shapes=[
            pltpu.VMEM((ROWS, COLS, NLAT), f32),
            pltpu.VMEM((3, ROWS, COLS, NLAT), f32),
            pltpu.VMEM((8, COLS, NLAT), f32),
            pltpu.VMEM((1, 12), jnp.int32),
            pltpu.VMEM((3, 12), f32),
            pltpu.VMEM((3, 12), f32),
            pltpu.VMEM((4, 8, 16, NLAT), f32),
            pltpu.VMEM((8, 16, NLAT), f32),
            pltpu.VMEM((3, 8, 16, NLAT), f32),
            pltpu.VMEM((8, 16, NLAT), f32),
            pltpu.VMEM((8, 16, NLAT), f32),
            pltpu.VMEM((8, 16, NLAT), f32),
            pltpu.VMEM((4, 16, NLAT), f32),
            pltpu.VMEM((4, 16, NLAT), f32),
            pltpu.VMEM((4, 56, NLAT), f32),
            pltpu.VMEM((4, 56, NLAT), f32),
            pltpu.VMEM((8, 128), f32),
            pltpu.VMEM((8, 8, 128), f32),
            pltpu.VMEM((8, 128), f32),
            pltpu.VMEM((8, 8, 128), f32),
            pltpu.VMEM((4, 24, 128), f32),
            pltpu.VMEM((4, 24, 128), f32),
            pltpu.VMEM((1024, 768), jnp.bfloat16),
            pltpu.VMEM((1024, 768), jnp.bfloat16),
            pltpu.VMEM((8, 3, 128), f32),
            pltpu.VMEM((32, 3, 128), f32),
            pltpu.VMEM((3, 128), f32),
            pltpu.VMEM((16, 3, 128), f32),
            pltpu.VMEM((4, 128), f32),
            pltpu.VMEM((8, 4, 128), f32),
            pltpu.VMEM((24, 128), f32),
            pltpu.VMEM((4, 24, 128), f32),
            pltpu.VMEM((768, 1024), jnp.bfloat16),
            pltpu.VMEM((768, 1024), jnp.bfloat16),
            pltpu.VMEM((8, 16, NLAT), f32),
            pltpu.VMEM((8, 16, NLAT), f32),
            pltpu.VMEM((8, 16, NLAT), f32),
            pltpu.VMEM((8, 16, NLAT), f32),
            pltpu.VMEM((3, 8, 16, NLAT), f32),
            pltpu.VMEM((3, 8, 16, NLAT), f32),
            pltpu.VMEM((3, 8, 16, NLAT), f32),
            pltpu.VMEM((3, 8, 16, NLAT), f32),
            pltpu.VMEM((3, 8, 16, NLAT), f32),
            pltpu.VMEM((3, 8, 16, NLAT), f32),
            pltpu.SemaphoreType.DMA((17,)),
            pltpu.SemaphoreType.DMA((17,)),
            pltpu.SemaphoreType.DMA((6,)),
        ],
        compiler_params=pltpu.CompilerParams(
            collective_id=0, has_side_effects=True, vmem_limit_bytes=62 * 1024 * 1024
        ),
    )(logvisc, displacement, ice_history, load_steps, site_cells.reshape(1, 12), observed, site_weight)
    half_momentum = momentum - 0.5 * gradient
    return logvisc + half_momentum, half_momentum, misfit


def solution(mesh):
    return jax.shard_map(
        body,
        mesh=mesh,
        in_specs=(
            P("rad", "lon", None),
            P("rad", "lon", None),
            P(None, "rad", "lon", None),
            P(None, "lon", None),
            P(),
            P("lon"),
            P(None, "lon"),
            P(None, "lon"),
        ),
        out_specs=(P("rad", "lon", None), P("rad", "lon", None), P()),
        check_vma=False,
    )
```

```python
import functools
import math

import jax
import jax.numpy as jnp
from jax import lax
from jax.experimental import pallas as pl
from jax.experimental.pallas import tpu as pltpu
from jax.sharding import PartitionSpec as P

MESH = pl.DeviceIdType.MESH
NR, NLON, NLAT = 96, 256, 512
ROWS = 12
COLS = 4
SCALE = 1.0 / math.sqrt(NLON * NLAT)
WAVE = [0.5 * (-1) ** k * (2.0 * math.pi) ** (2 * k + 1) / math.factorial(2 * k + 1) for k in range(6)]


def place():
    lon, rad = lax.axis_index("lon"), lax.axis_index("rad")
    return lon // 16, (rad // 4) * 8 + (lon // 2) % 8, lon % 2, rad % 4


def device(y, z, c, x):
    return (y * 16 + (z % 8) * 2 + c, (z // 8) * 4 + x)


def z_peer(i):
    y, z, c, x = place()
    z2 = (z + i) % 16
    return device(y, z2, c, x), z2


def plane_peer(i):
    y, z, c, x = place()
    x2, y2, c2 = (x + i % 4) % 4, (y + (i // 4) % 4) % 4, (c + i // 16) % 2
    return device(y2, z, c2, x2), x2, y2 * 2 + c2


def block_peer(i):
    y, z, c, x = place()
    y2, c2 = (y + i % 4) % 4, (c + i // 4) % 2
    return device(y2, z, c2, x), y2 * 2 + c2


def x_peer(i):
    y, z, c, x = place()
    x2 = (x + i) % 4
    return device(y, z, c, x2), x2


def repeat(first, last, step):
    for i in range(first, last):
        step(i)


def ring(offset, size):
    return min(offset % size, size - offset % size)


FAR_Z = sorted(range(1, 16), key=lambda i: -ring(i, 16))
NEAR_Z = [i for i in FAR_Z if ring(i, 16) <= 4]
FAR_PLANE = sorted(range(1, 32), key=lambda i: -(ring(i, 4) + ring(i // 4, 4) + 0.5 * (i // 16)))


def send(src, dst, ssem, rsem, target):
    pltpu.make_async_remote_copy(
        src_ref=src, dst_ref=dst, send_sem=ssem, recv_sem=rsem, device_id=target, device_id_type=MESH
    ).start()


def await_bytes(ref, sem):
    pltpu.make_async_copy(ref, ref, sem).wait()


def iota(shape, dim):
    return lax.broadcasted_iota(jnp.int32, shape, dim)


def next_lat(v):
    return pltpu.roll(v, NLAT - 1, v.ndim - 1)


def last_lat(v):
    return pltpu.roll(v, 1, v.ndim - 1)


def next_row(v):
    return pltpu.roll(v, 15, 0)


def last_row(v):
    return pltpu.roll(v, 1, 0)


def blocks_to_lanes(blocks):
    lane = iota((8, 128), 1)
    tiles = []
    for t in range(6):
        b = (128 * t) // 96
        first, second = 96 * b - 128 * t, 96 * (b + 1) - 128 * t
        low = pltpu.roll(blocks[b], first % 128, 1) if first % 128 else blocks[b]
        high = pltpu.roll(blocks[b + 1], second % 128, 1)
        tiles.append(jnp.where(lane < second, low, high))
    return tiles


def split(v):
    high = v.astype(jnp.bfloat16)
    return high, (v - high.astype(jnp.float32)).astype(jnp.bfloat16)


def kernel(
    lv_hbm, u_hbm, ice_hbm, steps_ref, cells_hbm, observed_hbm, weight_hbm,
    grad_ref, misfit_ref,
    lv_ref, u_ref, ice_ref, cells_ref, observed_ref, weight_ref,
    X, E, S1, QA, QO, QR, radS, radR, lonS, lonR,
    packet, gathered, block, sites, SB, RB, KH, KL,
    PB, C1R, C2S, C2R, C3S, C3R, SD, DR,
    TH, TL, AS, AA, AL, AO, UO, SO, UA, SA, UR, SR, ssem, rsem, isem,
):
    lon, rad = lax.axis_index("lon"), lax.axis_index("rad")
    y, z, c, x = place()
    own_block = y * 2 + c
    right, left = ((lon + 1) % 64, rad), ((lon + 63) % 64, rad)
    above, below = (lon, lax.min(rad + 1, 7)), (lon, lax.max(rad - 1, 0))

    barrier = pltpu.get_barrier_semaphore()

    def greet(target):
        pl.semaphore_signal(barrier, 1, device_id=target, device_id_type=MESH)

    has_above, has_below = rad < 7, rad > 0
    pl.when(has_above)(lambda: greet(above))
    pl.when(has_below)(lambda: greet(below))
    greet(right)
    greet(left)
    for i in NEAR_Z:
        greet(z_peer(i)[0])
    for i in FAR_PLANE:
        greet(plane_peer(i)[0])
    loads = [
        pltpu.make_async_copy(source, target, isem.at[k])
        for k, (source, target) in enumerate((
            (cells_hbm, cells_ref), (observed_hbm, observed_ref), (weight_hbm, weight_ref),
            (lv_hbm, lv_ref), (u_hbm, u_ref), (ice_hbm, ice_ref),
        ))
    ]
    for load in loads:
        load.start()
    for load in loads:
        load.wait()

    for f in range(4):
        for l in range(COLS):
            source = lv_ref[:, l, :] if f == 0 else u_ref[f - 1, :, l, :]
            X[f, l + 2, 0:ROWS, :] = source
            X[f, l + 2, ROWS:16, :] = jnp.zeros((16 - ROWS, NLAT), jnp.float32)
            radS[0, f * 4 + l : f * 4 + l + 1, :] = source[11:12, :]
            radS[1, f * 4 + l : f * 4 + l + 1, :] = source[0:1, :]
            if l == COLS - 1:
                lonS[0, f * ROWS : f * ROWS + ROWS, :] = source
            if l == 0:
                lonS[1, f * ROWS : f * ROWS + ROWS, :] = source
    packet[...] = jnp.zeros((8, 128), jnp.float32)
    packet[0:1, 0:12] = cells_ref[...].astype(jnp.float32)
    packet[1:4, 0:12] = observed_ref[...]
    packet[4:7, 0:12] = weight_ref[...]
    gathered[z % 8] = packet[...]
    nothing = jnp.zeros((16, NLAT), jnp.float32)

    @pl.when(rad == 7)
    def no_layer_above():
        radR[1] = nothing
        radR[3] = nothing

    @pl.when(rad == 0)
    def no_layer_below():
        radR[0] = nothing
        radR[2] = nothing

    pl.semaphore_wait(barrier, 41 + lax.min(rad, 1) + lax.min(7 - rad, 1))

    pl.when(has_above)(lambda: send(radS.at[0], radR.at[0], ssem.at[0], rsem.at[0], above))
    pl.when(has_below)(lambda: send(radS.at[1], radR.at[1], ssem.at[1], rsem.at[1], below))

    def send_record(i):
        target, unused = z_peer((i + 12) % 16)
        send(packet, gathered.at[z % 8], ssem.at[4], rsem.at[4], target)

    repeat(0, 4, send_record)
    repeat(5, 8, send_record)
    for side in (1 - c, c):
        target = (lax.rem(lon + 65 - 2 * side, 64), rad)
        send(lonS.at[side, pl.ds(0, 48)], lonR.at[side, pl.ds(0, 48)], ssem.at[2 + side], rsem.at[2 + side], target)

    row = iota((16, NLAT), 0)
    layer = jnp.where(row >= 14, row - 16, row)
    depth = (layer + rad * ROWS).astype(jnp.float32)
    wr = jnp.exp(4.0 * (depth - (NR - 1)) / NR)
    wr_next = jnp.exp(4.0 * (depth + 1.0 - (NR - 1)) / NR)
    own_row = row < ROWS
    wr_own = jnp.where(own_row, wr, 0.0)
    deep = layer + rad * ROWS
    face_ok = (row != 13) & (deep >= 0) & (deep < NR - 1)
    not_last = iota((16, NLAT), 1) < NLAT - 1
    is_top = jnp.where(rad == 7, 1.0, 0.0)

    await_bytes(gathered.at[pl.ds(0, 7)], rsem.at[4])
    record = gathered[0]
    for slot in range(1, 8):
        record = record + pltpu.roll(gathered[slot], 12 * slot, 1)
    block[...] = record
    sites[own_block] = record

    def send_block(i):
        target, unused = block_peer(i)
        send(block, sites.at[own_block], ssem.at[5], rsem.at[5], target)

    repeat(1, 8, send_block)

    await_bytes(lonR.at[0, pl.ds(0, 48)], rsem.at[2])
    await_bytes(lonR.at[1, pl.ds(0, 48)], rsem.at[3])
    for f in range(4):
        for side, p in ((0, 1), (1, 6)):
            X[f, p, 0:ROWS, :] = lonR[side, f * ROWS : f * ROWS + ROWS, :]
            X[f, p, ROWS:16, :] = jnp.zeros((16 - ROWS, NLAT), jnp.float32)
    pl.when(has_below)(lambda: await_bytes(radR.at[0], rsem.at[0]))
    pl.when(has_above)(lambda: await_bytes(radR.at[1], rsem.at[1]))
    for f in range(4):
        for l in range(COLS):
            X[f, l + 2, 15:16, :] = radR[0, f * 4 + l : f * 4 + l + 1, :]
            X[f, l + 2, 12:13, :] = radR[1, f * 4 + l : f * 4 + l + 1, :]

    def edge_lat(e):
        return jnp.where(not_last, 0.1 / (e + next_lat(e)), 0.0)

    def edge_rad(e):
        return jnp.where(face_ok, 0.1 / (e + next_row(e)), 0.0)

    for p in range(1, 7):
        E[p] = jnp.exp(X[0, p])
    for p in range(2, 6):
        QA[p] = edge_lat(E[p])
        QR[p] = edge_rad(E[p])
    for p in range(1, 6):
        QO[p] = 0.1 / (E[p] + E[p + 1])
    load_1, load_2 = ice_ref[steps_ref[0]], ice_ref[steps_ref[1]]
    for f in range(3):
        for p in range(2, 6):
            u = X[f + 1, p]
            flux = QA[p] * (next_lat(u) - u)
            rise = QR[p] * (next_row(u) - u)
            total = u + (flux - last_lat(flux)) + (rise - last_row(rise))
            total = total + QO[p] * (X[f + 1, p + 1] - u) + QO[p - 1] * (X[f + 1, p - 1] - u)
            if f == 0:
                pressed = jnp.broadcast_to(load_1[p - 2 : p - 1, :], (16, NLAT)) * is_top
                total = total - jnp.where(row == ROWS - 1, pressed, 0.0)
            S1[f, p] = total

    columns = []
    for f in range(3):
        columns.append([jnp.zeros((1, NLAT), jnp.float32) for unused in range(8)])

    def column_sum(v):
        return jnp.sum(v, axis=0, keepdims=True)

    for p in range(2, 6):
        slope = QR[p] * (wr_next - wr)
        factor = jnp.where(own_row, wr + slope - last_row(slope), 0.0)
        along = wr_own * QA[p]
        for f in range(3):
            s = S1[f, p]
            flux = column_sum(along * (next_lat(s) - s))
            columns[f][p] = columns[f][p] + column_sum(factor * s) + (flux - last_lat(flux))
    for p in range(1, 6):
        across = wr_own * QO[p]
        for f in range(3):
            if p == 1:
                flow = column_sum(across * S1[f, 2])
            elif p == 5:
                flow = -column_sum(across * S1[f, 5])
            else:
                flow = column_sum(across * (S1[f, p + 1] - S1[f, p]))
            columns[f][p] = columns[f][p] + flow
            columns[f][p + 1] = columns[f][p + 1] - flow
    for p in range(2, 6):
        columns[0][p] = columns[0][p] - load_2[p - 2 : p - 1, :] * is_top
    for f in range(3):
        for p in range(8):
            for band in range(4):
                SB[band, f * 8 + p : f * 8 + p + 1, :] = columns[f][p][:, band * 128 : band * 128 + 128]
    RB[x] = SB[x]

    def send_band(i):
        target, x2 = x_peer(i)
        send(SB.at[x2], RB.at[x], ssem.at[6], rsem.at[6], target)

    repeat(1, 4, send_band)

    for f in range(3):
        for l in range(COLS):
            radS[2, f * 4 + l : f * 4 + l + 1, :] = S1[f, l + 2, 11:12, :]
            radS[3, f * 4 + l : f * 4 + l + 1, :] = S1[f, l + 2, 0:1, :]
    for l in range(COLS):
        radS[2, 12 + l : 13 + l, :] = X[0, l + 2, 10:11, :]
        radS[3, 12 + l : 13 + l, :] = X[0, l + 2, 1:2, :]
    for side, edge, inner in ((2, 5, 4), (3, 2, 3)):
        for f in range(3):
            lonS[side, f * ROWS : f * ROWS + ROWS, :] = S1[f, edge, 0:ROWS, :]
        lonS[side, 36:48, :] = X[0, inner, 0:ROWS, :]
        lonS[side, 48:52, :] = X[0, edge, ROWS:16, :]
        lonS[side, 52:56, :] = jnp.zeros((4, NLAT), jnp.float32)
    pl.when(has_above)(lambda: send(radS.at[2], radR.at[2], ssem.at[7], rsem.at[7], above))
    pl.when(has_below)(lambda: send(radS.at[3], radR.at[3], ssem.at[8], rsem.at[8], below))
    send(lonS.at[2], lonR.at[2], ssem.at[9], rsem.at[9], right)
    send(lonS.at[3], lonR.at[3], ssem.at[10], rsem.at[10], left)

    await_bytes(sites.at[pl.ds(0, 7)], rsem.at[5])
    tiles = blocks_to_lanes([sites[b] for b in range(8)])
    theta = (iota((128, 128), 0) + x * 128).astype(jnp.float32)
    theta = math.pi * (theta + 0.5) / NLAT
    cell_cos, cell_sin = jnp.cos(theta), jnp.sin(theta)
    plane_lon = (iota((8, 128), 0) + (lon * COLS - 2)).astype(jnp.float32)
    for t in range(6):
        cell = jnp.broadcast_to(tiles[t][0:1, :], (8, 128))
        site_lon = jnp.floor(cell * (1.0 / NLAT))
        site_theta = math.pi * (cell - NLAT * site_lon + 0.5) / NLAT
        up = jnp.cos(site_theta)
        side = jnp.sin(site_theta) * jnp.cos(2.0 * math.pi * (site_lon - plane_lon) / NLON)
        for p in range(8):
            cosine = cell_cos * up[0:1, :] + cell_sin * side[p : p + 1, :]
            chord = 2.0 - 2.0 * cosine
            turns = chord * (40.0 / (2.0 * math.pi))
            turns = 0.25 - jnp.abs(turns - jnp.round(turns))
            squared = turns * turns
            wave = jnp.full_like(squared, WAVE[5])
            for k in range(4, -1, -1):
                wave = wave * squared + WAVE[k]
            value = 1.0 / (1.0 + chord * 10.0) + wave * turns
            high, low = split(value)
            KH[p * 128 : p * 128 + 128, t * 128 : t * 128 + 128] = high
            KL[p * 128 : p * 128 + 128, t * 128 : t * 128 + 128] = low

    await_bytes(RB.at[pl.ds(0, 3)], rsem.at[6])
    band = (RB[0] + RB[1]) + (RB[2] + RB[3])
    place_of = iota((24, 128), 0) % 8
    wide = jnp.concatenate([jnp.where(place_of == p, band, 0.0) for p in range(1, 7)], axis=1)
    high, low = split(wide)
    dot = functools.partial(jnp.dot, preferred_element_type=jnp.float32)
    both = jnp.concatenate([high.astype(jnp.float32), low.astype(jnp.float32)], axis=0).astype(jnp.bfloat16)
    parts = dot(both, KH[128:896])
    parts = parts[0:24] + parts[24:48] + dot(high, KL[128:896])
    row8 = iota((8, 6 * 128), 0)
    pred = jnp.zeros((8, 6 * 128), jnp.float32)
    for f in range(3):
        summed = jnp.sum(parts[f * 8 : f * 8 + 8, :], axis=0, keepdims=True) * SCALE
        pred = jnp.where(row8 == f, jnp.broadcast_to(summed, pred.shape), pred)
    for half in range(2):
        for f in range(3):
            PB[half, :, f * 384 : f * 384 + 384] = pred[f : f + 1, half * 384 : half * 384 + 384]
    C1R[x * 8 + own_block] = PB[c]

    def send_piece(i):
        target, unused, b2 = plane_peer(i)
        send(PB.at[b2 % 2], C1R.at[x * 8 + own_block], ssem.at[13], rsem.at[13], target)

    for i in FAR_PLANE:
        send_piece(i)
    await_bytes(C1R.at[pl.ds(0, 31)], rsem.at[13])
    summed = jnp.sum(C1R[...], axis=0)
    C2S[...] = summed
    C2R[z] = summed

    def send_sum(i):
        target, unused = z_peer(i)
        send(C2S, C2R.at[z], ssem.at[14], rsem.at[14], target)

    for i in FAR_Z:
        send_sum(i)

    pl.when(has_below)(lambda: await_bytes(radR.at[2], rsem.at[7]))
    pl.when(has_above)(lambda: await_bytes(radR.at[3], rsem.at[8]))
    await_bytes(lonR.at[2], rsem.at[9])
    await_bytes(lonR.at[3], rsem.at[10])
    for f in range(3):
        for l in range(COLS):
            S1[f, l + 2, 15:16, :] = radR[2, f * 4 + l : f * 4 + l + 1, :]
            S1[f, l + 2, 12:13, :] = radR[3, f * 4 + l : f * 4 + l + 1, :]
    for l in range(COLS):
        X[0, l + 2, 14:15, :] = radR[2, 12 + l : 13 + l, :]
        X[0, l + 2, 13:14, :] = radR[3, 12 + l : 13 + l, :]
    for side, far, near in ((2, 0, 1), (3, 7, 6)):
        for f in range(3):
            S1[f, near, 0:ROWS, :] = lonR[side, f * ROWS : f * ROWS + ROWS, :]
            S1[f, near, ROWS:16, :] = jnp.zeros((16 - ROWS, NLAT), jnp.float32)
        X[0, far, 0:ROWS, :] = lonR[side, 36:48, :]
        X[0, far, ROWS:16, :] = jnp.zeros((16 - ROWS, NLAT), jnp.float32)
        X[0, near, ROWS:16, :] = lonR[side, 48:52, :]
    for p in range(8):
        E[p] = jnp.exp(X[0, p])
    for p in range(1, 7):
        QA[p] = edge_lat(E[p])
        QR[p] = edge_rad(E[p])
    for p in range(7):
        QO[p] = 0.1 / (E[p] + E[p + 1])
    for p in range(1, 7):
        slope = QR[p] * (wr_next - wr)
        AS[p] = wr + slope - last_row(slope)
        along = QA[p] * wr
        AA[p] = along
        AL[p] = last_lat(along)
    for p in range(7):
        AO[p] = QO[p] * wr
    for f in range(3):
        for p in range(1, 6):
            u, s, square = X[f + 1, p], S1[f, p], QO[p] * QO[p]
            UO[f, p] = square * (X[f + 1, p + 1] - u)
            SO[f, p] = square * wr * (S1[f, p + 1] - s)
            if p > 1:
                square = QA[p] * QA[p]
                UA[f, p] = square * (next_lat(u) - u)
                SA[f, p] = square * wr * (next_lat(s) - s)
                square = QR[p] * QR[p]
                UR[f, p] = square * (next_row(u) - u)
                SR[f, p] = square * (wr_next - wr) * (next_row(s) - s)
    for t in range(6):
        for p in range(8):
            TH[t * 128 : t * 128 + 128, p * 128 : p * 128 + 128] = KH[p * 128 : p * 128 + 128, t * 128 : t * 128 + 128].T
            TL[t * 128 : t * 128 + 128, p * 128 : p * 128 + 128] = KL[p * 128 : p * 128 + 128, t * 128 : t * 128 + 128].T

    record = jnp.where(c == 0, jnp.concatenate(tiles[0:3], axis=1), jnp.concatenate(tiles[3:6], axis=1))
    row_of = iota((8, 384), 0)
    weight = jnp.where(row_of < 3, pltpu.roll(record, 4, 0), 0.0)
    aim = pltpu.roll(record, 7, 0)

    await_bytes(C2R.at[pl.ds(0, 15)], rsem.at[14])
    total = jnp.sum(C2R[...], axis=0)
    predicted = jnp.concatenate(
        [total[:, f * 384 : f * 384 + 384] for f in range(3)] + [jnp.zeros((5, 384), jnp.float32)], axis=0
    )
    weighted = weight * (predicted - aim)
    squares = jnp.broadcast_to(jnp.sum(weighted * weighted, axis=0, keepdims=True), (8, 384))
    pulled = jnp.where(row_of == 3, squares, weight * weighted)
    C3S[...] = pulled[0:4]
    C3R[c] = pulled[0:4]
    send(C3S, C3R.at[c], ssem.at[15], rsem.at[15], device(y, z, 1 - c, x))
    await_bytes(C3R.at[0], rsem.at[15])
    pull = jnp.concatenate([C3R[0], C3R[1]], axis=1)
    pull = jnp.concatenate([pull, jnp.zeros((4, 768), jnp.float32)], axis=0)
    high, low = split(pull)
    both = jnp.concatenate([high, low], axis=0)

    first = dot(both, TH[...])
    adjoint = (first[0:8] + first[8:16] + dot(both, TL[...])[0:8]) * SCALE
    for f in range(3):
        for p in range(8):
            SD[f * 8 + p : f * 8 + p + 1, :] = adjoint[f : f + 1, p * 128 : p * 128 + 128]
    DR[x] = SD[...]

    def send_adjoint(i):
        target, unused = x_peer(i)
        send(SD, DR.at[x], ssem.at[16], rsem.at[16], target)

    repeat(1, 4, send_adjoint)
    misfit_ref[0] = jnp.sum(C3R[0, 3:4, :] + C3R[1, 3:4, :]) / (3.0 * 768.0)
    await_bytes(DR.at[pl.ds(0, 3)], rsem.at[16])

    faces_a = [jnp.zeros((16, NLAT), jnp.float32) for unused in range(8)]
    faces_r = [jnp.zeros((16, NLAT), jnp.float32) for unused in range(8)]
    faces_o = [jnp.zeros((16, NLAT), jnp.float32) for unused in range(8)]

    def spread(v, p):
        return jnp.broadcast_to(v[p : p + 1, :], (16, NLAT))

    for f in range(3):
        surface = jnp.concatenate([DR[band, f * 8 : f * 8 + 8, :] for band in range(4)], axis=1)
        step = next_lat(surface) - surface
        step_before = last_lat(step)
        beside = [spread(surface, p + 1) - spread(surface, p) for p in range(7)]
        a1 = [None] * 8
        for p in range(1, 7):
            a1[p] = (
                AS[p] * spread(surface, p) + AA[p] * spread(step, p) - AL[p] * spread(step_before, p)
                + AO[p] * beside[p] - AO[p - 1] * beside[p - 1]
            )
        for p in range(1, 6):
            faces_o[p] = faces_o[p] + UO[f, p] * (a1[p + 1] - a1[p]) + SO[f, p] * beside[p]
            if p > 1:
                faces_a[p] = faces_a[p] + UA[f, p] * (next_lat(a1[p]) - a1[p]) + SA[f, p] * spread(step, p)
                faces_r[p] = faces_r[p] + UR[f, p] * (next_row(a1[p]) - a1[p]) + SR[f, p] * spread(surface, p)
    for p in range(2, 6):
        along, upward = faces_a[p], faces_r[p]
        whole = (along + last_lat(along)) + (upward + last_row(upward)) + (faces_o[p] + faces_o[p - 1])
        result = 10.0 * E[p] * whole + 0.1 * X[0, p]
        grad_ref[:, p - 2, :] = result[0:ROWS, :]

    pl.when(has_above)(lambda: await_bytes(radS.at[0], ssem.at[0]))
    pl.when(has_below)(lambda: await_bytes(radS.at[1], ssem.at[1]))
    pl.when(has_above)(lambda: await_bytes(radS.at[2], ssem.at[7]))
    pl.when(has_below)(lambda: await_bytes(radS.at[3], ssem.at[8]))
    for k, ref in ((2, lonS.at[0, pl.ds(0, 48)]), (3, lonS.at[1, pl.ds(0, 48)]), (4, gathered.at[pl.ds(0, 7)]),
                   (5, sites.at[pl.ds(0, 7)]), (6, RB.at[pl.ds(0, 3)]), (9, lonS.at[2]), (10, lonS.at[3]),
                   (13, C1R.at[pl.ds(0, 31)]), (14, C2R.at[pl.ds(0, 15)]),
                   (15, C3S), (16, DR.at[pl.ds(0, 3)])):
        await_bytes(ref, ssem.at[k])


def body(logvisc, momentum, displacement, ice_history, load_steps, site_cells, observed, site_weight):
    f32 = jnp.float32
    vmem = pl.BlockSpec(memory_space=pltpu.VMEM)
    smem = pl.BlockSpec(memory_space=pltpu.SMEM)
    hbm = pl.BlockSpec(memory_space=pltpu.HBM)
    gradient, misfit = pl.pallas_call(
        kernel,
        out_shape=(
            pltpu.VMEM((ROWS, COLS, NLAT), f32),
            jax.ShapeDtypeStruct((1,), f32),
        ),
        in_specs=[hbm, hbm, hbm, smem, hbm, hbm, hbm],
        out_specs=(vmem, smem),
        scratch_shapes=[
            pltpu.VMEM((ROWS, COLS, NLAT), f32),
            pltpu.VMEM((3, ROWS, COLS, NLAT), f32),
            pltpu.VMEM((8, COLS, NLAT), f32),
            pltpu.VMEM((1, 12), jnp.int32),
            pltpu.VMEM((3, 12), f32),
            pltpu.VMEM((3, 12), f32),
            pltpu.VMEM((4, 8, 16, NLAT), f32),
            pltpu.VMEM((8, 16, NLAT), f32),
            pltpu.VMEM((3, 8, 16, NLAT), f32),
            pltpu.VMEM((8, 16, NLAT), f32),
            pltpu.VMEM((8, 16, NLAT), f32),
            pltpu.VMEM((8, 16, NLAT), f32),
            pltpu.VMEM((4, 16, NLAT), f32),
            pltpu.VMEM((4, 16, NLAT), f32),
            pltpu.VMEM((4, 56, NLAT), f32),
            pltpu.VMEM((4, 56, NLAT), f32),
            pltpu.VMEM((8, 128), f32),
            pltpu.VMEM((8, 8, 128), f32),
            pltpu.VMEM((8, 128), f32),
            pltpu.VMEM((8, 8, 128), f32),
            pltpu.VMEM((4, 24, 128), f32),
            pltpu.VMEM((4, 24, 128), f32),
            pltpu.VMEM((1024, 768), jnp.bfloat16),
            pltpu.VMEM((1024, 768), jnp.bfloat16),
            pltpu.VMEM((2, 1, 1152), f32),
            pltpu.VMEM((32, 1, 1152), f32),
            pltpu.VMEM((1, 1152), f32),
            pltpu.VMEM((16, 1, 1152), f32),
            pltpu.VMEM((4, 384), f32),
            pltpu.VMEM((2, 4, 384), f32),
            pltpu.VMEM((24, 128), f32),
            pltpu.VMEM((4, 24, 128), f32),
            pltpu.VMEM((768, 1024), jnp.bfloat16),
            pltpu.VMEM((768, 1024), jnp.bfloat16),
            pltpu.VMEM((8, 16, NLAT), f32),
            pltpu.VMEM((8, 16, NLAT), f32),
            pltpu.VMEM((8, 16, NLAT), f32),
            pltpu.VMEM((8, 16, NLAT), f32),
            pltpu.VMEM((3, 8, 16, NLAT), f32),
            pltpu.VMEM((3, 8, 16, NLAT), f32),
            pltpu.VMEM((3, 8, 16, NLAT), f32),
            pltpu.VMEM((3, 8, 16, NLAT), f32),
            pltpu.VMEM((3, 8, 16, NLAT), f32),
            pltpu.VMEM((3, 8, 16, NLAT), f32),
            pltpu.SemaphoreType.DMA((17,)),
            pltpu.SemaphoreType.DMA((17,)),
            pltpu.SemaphoreType.DMA((6,)),
        ],
        compiler_params=pltpu.CompilerParams(
            collective_id=0, has_side_effects=True, vmem_limit_bytes=62 * 1024 * 1024
        ),
    )(logvisc, displacement, ice_history, load_steps, site_cells.reshape(1, 12), observed, site_weight)
    half_momentum = momentum - 0.5 * gradient
    return logvisc + half_momentum, half_momentum, misfit


def solution(mesh):
    return jax.shard_map(
        body,
        mesh=mesh,
        in_specs=(
            P("rad", "lon", None),
            P("rad", "lon", None),
            P(None, "rad", "lon", None),
            P(None, "lon", None),
            P(),
            P("lon"),
            P(None, "lon"),
            P(None, "lon"),
        ),
        out_specs=(P("rad", "lon", None), P("rad", "lon", None), P()),
        check_vma=False,
    )
```

```python
import functools
import math

import jax
import jax.numpy as jnp
from jax import lax
from jax.experimental import pallas as pl
from jax.experimental.pallas import tpu as pltpu
from jax.sharding import PartitionSpec as P

MESH = pl.DeviceIdType.MESH
NR, NLON, NLAT = 96, 256, 512
ROWS = 12
COLS = 4
SCALE = 1.0 / math.sqrt(NLON * NLAT)
WAVE = [0.5 * (-1) ** k * (2.0 * math.pi) ** (2 * k + 1) / math.factorial(2 * k + 1) for k in range(6)]


def place():
    lon, rad = lax.axis_index("lon"), lax.axis_index("rad")
    return lon // 16, (rad // 4) * 8 + (lon // 2) % 8, lon % 2, rad % 4


def device(y, z, c, x):
    return (y * 16 + (z % 8) * 2 + c, (z // 8) * 4 + x)


def z_peer(i):
    y, z, c, x = place()
    z2 = (z + i) % 16
    return device(y, z2, c, x), z2


def plane_peer(i):
    y, z, c, x = place()
    x2, y2, c2 = (x + i % 4) % 4, (y + (i // 4) % 4) % 4, (c + i // 16) % 2
    return device(y2, z, c2, x2), x2, y2 * 2 + c2


def block_peer(i):
    y, z, c, x = place()
    y2, c2 = (y + i % 4) % 4, (c + i // 4) % 2
    return device(y2, z, c2, x), y2 * 2 + c2


def x_peer(i):
    y, z, c, x = place()
    x2 = (x + i) % 4
    return device(y, z, c, x2), x2


def repeat(first, last, step):
    for i in range(first, last):
        step(i)


def ring(offset, size):
    return min(offset % size, size - offset % size)


FAR_Z = sorted(range(1, 16), key=lambda i: -ring(i, 16))
NEAR_Z = [i for i in FAR_Z if ring(i, 16) <= 4]
FAR_PLANE = sorted(range(1, 32), key=lambda i: -(ring(i, 4) + ring(i // 4, 4) + 0.5 * (i // 16)))


def send(src, dst, ssem, rsem, target):
    pltpu.make_async_remote_copy(
        src_ref=src, dst_ref=dst, send_sem=ssem, recv_sem=rsem, device_id=target, device_id_type=MESH
    ).start()


def await_bytes(ref, sem):
    pltpu.make_async_copy(ref, ref, sem).wait()


def iota(shape, dim):
    return lax.broadcasted_iota(jnp.int32, shape, dim)


def next_lat(v):
    return pltpu.roll(v, NLAT - 1, v.ndim - 1)


def last_lat(v):
    return pltpu.roll(v, 1, v.ndim - 1)


def next_row(v):
    return pltpu.roll(v, 15, 0)


def last_row(v):
    return pltpu.roll(v, 1, 0)


def blocks_to_lanes(blocks):
    lane = iota((8, 128), 1)
    tiles = []
    for t in range(6):
        b = (128 * t) // 96
        first, second = 96 * b - 128 * t, 96 * (b + 1) - 128 * t
        low = pltpu.roll(blocks[b], first % 128, 1) if first % 128 else blocks[b]
        high = pltpu.roll(blocks[b + 1], second % 128, 1)
        tiles.append(jnp.where(lane < second, low, high))
    return tiles


def split(v):
    high = v.astype(jnp.bfloat16)
    return high, (v - high.astype(jnp.float32)).astype(jnp.bfloat16)


def kernel(
    lv_hbm, u_hbm, ice_hbm, steps_ref, cells_hbm, observed_hbm, weight_hbm,
    grad_ref, misfit_ref,
    lv_ref, u_ref, ice_ref, cells_ref, observed_ref, weight_ref,
    X, E, S1, QA, QO, QR, radS, radR, lonS, lonR,
    packet, gathered, block, sites, SB, RB, KH, KL,
    PB, C1R, C2S, C2R, C3S, C3R, SD, DR,
    TH, TL, AS, AA, AL, AO, UO, SO, UA, SA, UR, SR, ssem, rsem, isem,
):
    lon, rad = lax.axis_index("lon"), lax.axis_index("rad")
    y, z, c, x = place()
    own_block = y * 2 + c
    right, left = ((lon + 1) % 64, rad), ((lon + 63) % 64, rad)
    above, below = (lon, lax.min(rad + 1, 7)), (lon, lax.max(rad - 1, 0))

    barrier = pltpu.get_barrier_semaphore()

    def greet(target):
        pl.semaphore_signal(barrier, 1, device_id=target, device_id_type=MESH)

    has_above, has_below = rad < 7, rad > 0
    pl.when(has_above)(lambda: greet(above))
    pl.when(has_below)(lambda: greet(below))
    greet(right)
    greet(left)
    for i in NEAR_Z:
        greet(z_peer(i)[0])
    for i in FAR_PLANE:
        greet(plane_peer(i)[0])
    loads = [
        pltpu.make_async_copy(source, target, isem.at[k])
        for k, (source, target) in enumerate((
            (cells_hbm, cells_ref), (observed_hbm, observed_ref), (weight_hbm, weight_ref),
            (lv_hbm, lv_ref), (u_hbm, u_ref), (ice_hbm, ice_ref),
        ))
    ]
    for load in loads:
        load.start()
    for load in loads:
        load.wait()

    for f in range(4):
        for l in range(COLS):
            source = lv_ref[:, l, :] if f == 0 else u_ref[f - 1, :, l, :]
            X[f, l + 2, 0:ROWS, :] = source
            X[f, l + 2, ROWS:16, :] = jnp.zeros((16 - ROWS, NLAT), jnp.float32)
            radS[0, f * 4 + l : f * 4 + l + 1, :] = source[11:12, :]
            radS[1, f * 4 + l : f * 4 + l + 1, :] = source[0:1, :]
            if l == COLS - 1:
                lonS[0, f * ROWS : f * ROWS + ROWS, :] = source
            if l == 0:
                lonS[1, f * ROWS : f * ROWS + ROWS, :] = source
    packet[...] = jnp.zeros((8, 128), jnp.float32)
    packet[0:1, 0:12] = cells_ref[...].astype(jnp.float32)
    packet[1:4, 0:12] = observed_ref[...]
    packet[4:7, 0:12] = weight_ref[...]
    gathered[z % 8] = packet[...]
    nothing = jnp.zeros((16, NLAT), jnp.float32)

    @pl.when(rad == 7)
    def no_layer_above():
        radR[1] = nothing
        radR[3] = nothing

    @pl.when(rad == 0)
    def no_layer_below():
        radR[0] = nothing
        radR[2] = nothing

    pl.semaphore_wait(barrier, 41 + lax.min(rad, 1) + lax.min(7 - rad, 1))

    pl.when(has_above)(lambda: send(radS.at[0], radR.at[0], ssem.at[0], rsem.at[0], above))
    pl.when(has_below)(lambda: send(radS.at[1], radR.at[1], ssem.at[1], rsem.at[1], below))

    def send_record(i):
        target, unused = z_peer((i + 12) % 16)
        send(packet, gathered.at[z % 8], ssem.at[4], rsem.at[4], target)

    repeat(0, 4, send_record)
    repeat(5, 8, send_record)
    for side in (1 - c, c):
        target = (lax.rem(lon + 65 - 2 * side, 64), rad)
        send(lonS.at[side, pl.ds(0, 48)], lonR.at[side, pl.ds(0, 48)], ssem.at[2 + side], rsem.at[2 + side], target)

    row = iota((16, NLAT), 0)
    layer = jnp.where(row >= 14, row - 16, row)
    depth = (layer + rad * ROWS).astype(jnp.float32)
    wr = jnp.exp(4.0 * (depth - (NR - 1)) / NR)
    wr_next = jnp.exp(4.0 * (depth + 1.0 - (NR - 1)) / NR)
    own_row = row < ROWS
    wr_own = jnp.where(own_row, wr, 0.0)
    deep = layer + rad * ROWS
    face_ok = (row != 13) & (deep >= 0) & (deep < NR - 1)
    not_last = iota((16, NLAT), 1) < NLAT - 1
    is_top = jnp.where(rad == 7, 1.0, 0.0)

    def edge_lat(e):
        return jnp.where(not_last, 0.1 / (e + next_lat(e)), 0.0)

    for p in range(2, 6):
        E[p] = jnp.exp(X[0, p])
        QA[p] = edge_lat(E[p])
        for f in range(3):
            u = X[f + 1, p]
            flux = QA[p] * (next_lat(u) - u)
            S1[f, p] = u + (flux - last_lat(flux))
    for p in range(2, 5):
        QO[p] = 0.1 / (E[p] + E[p + 1])
        for f in range(3):
            flow = QO[p] * (X[f + 1, p + 1] - X[f + 1, p])
            S1[f, p] = S1[f, p] + flow
            S1[f, p + 1] = S1[f, p + 1] - flow

    await_bytes(gathered.at[pl.ds(0, 7)], rsem.at[4])
    record = gathered[0]
    for slot in range(1, 8):
        record = record + pltpu.roll(gathered[slot], 12 * slot, 1)
    block[...] = record
    sites[own_block] = record

    def send_block(i):
        target, unused = block_peer(i)
        send(block, sites.at[own_block], ssem.at[5], rsem.at[5], target)

    repeat(1, 8, send_block)

    await_bytes(lonR.at[0, pl.ds(0, 48)], rsem.at[2])
    await_bytes(lonR.at[1, pl.ds(0, 48)], rsem.at[3])
    for f in range(4):
        for side, p in ((0, 1), (1, 6)):
            X[f, p, 0:ROWS, :] = lonR[side, f * ROWS : f * ROWS + ROWS, :]
            X[f, p, ROWS:16, :] = jnp.zeros((16 - ROWS, NLAT), jnp.float32)
    pl.when(has_below)(lambda: await_bytes(radR.at[0], rsem.at[0]))
    pl.when(has_above)(lambda: await_bytes(radR.at[1], rsem.at[1]))
    for f in range(4):
        for l in range(COLS):
            X[f, l + 2, 15:16, :] = radR[0, f * 4 + l : f * 4 + l + 1, :]
            X[f, l + 2, 12:13, :] = radR[1, f * 4 + l : f * 4 + l + 1, :]

    def edge_rad(e):
        return jnp.where(face_ok, 0.1 / (e + next_row(e)), 0.0)

    for p in range(1, 7):
        E[p] = jnp.exp(X[0, p])
    for p in range(2, 6):
        QR[p] = edge_rad(E[p])
    for p in (1, 5):
        QO[p] = 0.1 / (E[p] + E[p + 1])
    load_1, load_2 = ice_ref[steps_ref[0]], ice_ref[steps_ref[1]]
    for f in range(3):
        for p in range(2, 6):
            u = X[f + 1, p]
            rise = QR[p] * (next_row(u) - u)
            total = S1[f, p] + (rise - last_row(rise))
            if p == 2:
                total = total + QO[1] * (X[f + 1, 1] - u)
            if p == 5:
                total = total + QO[5] * (X[f + 1, 6] - u)
            if f == 0:
                pressed = jnp.broadcast_to(load_1[p - 2 : p - 1, :], (16, NLAT)) * is_top
                total = total - jnp.where(row == ROWS - 1, pressed, 0.0)
            S1[f, p] = total

    columns = []
    for f in range(3):
        columns.append([jnp.zeros((1, NLAT), jnp.float32) for unused in range(8)])

    def column_sum(v):
        return jnp.sum(v, axis=0, keepdims=True)

    for p in range(2, 6):
        slope = QR[p] * (wr_next - wr)
        factor = jnp.where(own_row, wr + slope - last_row(slope), 0.0)
        along = wr_own * QA[p]
        for f in range(3):
            s = S1[f, p]
            flux = column_sum(along * (next_lat(s) - s))
            columns[f][p] = columns[f][p] + column_sum(factor * s) + (flux - last_lat(flux))
    for p in range(1, 6):
        across = wr_own * QO[p]
        for f in range(3):
            if p == 1:
                flow = column_sum(across * S1[f, 2])
            elif p == 5:
                flow = -column_sum(across * S1[f, 5])
            else:
                flow = column_sum(across * (S1[f, p + 1] - S1[f, p]))
            columns[f][p] = columns[f][p] + flow
            columns[f][p + 1] = columns[f][p + 1] - flow
    for p in range(2, 6):
        columns[0][p] = columns[0][p] - load_2[p - 2 : p - 1, :] * is_top
    for f in range(3):
        for p in range(8):
            for band in range(4):
                SB[band, f * 8 + p : f * 8 + p + 1, :] = columns[f][p][:, band * 128 : band * 128 + 128]
    RB[x] = SB[x]

    def send_band(i):
        target, x2 = x_peer(i)
        send(SB.at[x2], RB.at[x], ssem.at[6], rsem.at[6], target)

    repeat(1, 4, send_band)

    for f in range(3):
        for l in range(COLS):
            radS[2, f * 4 + l : f * 4 + l + 1, :] = S1[f, l + 2, 11:12, :]
            radS[3, f * 4 + l : f * 4 + l + 1, :] = S1[f, l + 2, 0:1, :]
    for l in range(COLS):
        radS[2, 12 + l : 13 + l, :] = X[0, l + 2, 10:11, :]
        radS[3, 12 + l : 13 + l, :] = X[0, l + 2, 1:2, :]
    for side, edge, inner in ((2, 5, 4), (3, 2, 3)):
        for f in range(3):
            lonS[side, f * ROWS : f * ROWS + ROWS, :] = S1[f, edge, 0:ROWS, :]
        lonS[side, 36:48, :] = X[0, inner, 0:ROWS, :]
        lonS[side, 48:52, :] = X[0, edge, ROWS:16, :]
        lonS[side, 52:56, :] = jnp.zeros((4, NLAT), jnp.float32)
    pl.when(has_above)(lambda: send(radS.at[2], radR.at[2], ssem.at[7], rsem.at[7], above))
    pl.when(has_below)(lambda: send(radS.at[3], radR.at[3], ssem.at[8], rsem.at[8], below))
    send(lonS.at[2], lonR.at[2], ssem.at[9], rsem.at[9], right)
    send(lonS.at[3], lonR.at[3], ssem.at[10], rsem.at[10], left)

    await_bytes(sites.at[pl.ds(0, 7)], rsem.at[5])
    tiles = blocks_to_lanes([sites[b] for b in range(8)])
    theta = (iota((128, 128), 0) + x * 128).astype(jnp.float32)
    theta = math.pi * (theta + 0.5) / NLAT
    cell_cos, cell_sin = jnp.cos(theta), jnp.sin(theta)
    plane_lon = (iota((8, 128), 0) + (lon * COLS - 2)).astype(jnp.float32)
    for t in range(6):
        cell = jnp.broadcast_to(tiles[t][0:1, :], (8, 128))
        site_lon = jnp.floor(cell * (1.0 / NLAT))
        site_theta = math.pi * (cell - NLAT * site_lon + 0.5) / NLAT
        up = jnp.cos(site_theta)
        side = jnp.sin(site_theta) * jnp.cos(2.0 * math.pi * (site_lon - plane_lon) / NLON)
        for p in range(8):
            cosine = cell_cos * up[0:1, :] + cell_sin * side[p : p + 1, :]
            chord = 2.0 - 2.0 * cosine
            turns = chord * (40.0 / (2.0 * math.pi))
            turns = 0.25 - jnp.abs(turns - jnp.round(turns))
            squared = turns * turns
            wave = jnp.full_like(squared, WAVE[5])
            for k in range(4, -1, -1):
                wave = wave * squared + WAVE[k]
            value = 1.0 / (1.0 + chord * 10.0) + wave * turns
            high, low = split(value)
            KH[p * 128 : p * 128 + 128, t * 128 : t * 128 + 128] = high
            KL[p * 128 : p * 128 + 128, t * 128 : t * 128 + 128] = low

    await_bytes(RB.at[pl.ds(0, 3)], rsem.at[6])
    band = (RB[0] + RB[1]) + (RB[2] + RB[3])
    place_of = iota((24, 128), 0) % 8
    wide = jnp.concatenate([jnp.where(place_of == p, band, 0.0) for p in range(1, 7)], axis=1)
    high, low = split(wide)
    dot = functools.partial(jnp.dot, preferred_element_type=jnp.float32)
    both = jnp.concatenate([high.astype(jnp.float32), low.astype(jnp.float32)], axis=0).astype(jnp.bfloat16)
    parts = dot(both, KH[128:896])
    parts = parts[0:24] + parts[24:48] + dot(high, KL[128:896])
    row8 = iota((8, 6 * 128), 0)
    pred = jnp.zeros((8, 6 * 128), jnp.float32)
    for f in range(3):
        summed = jnp.sum(parts[f * 8 : f * 8 + 8, :], axis=0, keepdims=True) * SCALE
        pred = jnp.where(row8 == f, jnp.broadcast_to(summed, pred.shape), pred)
    for half in range(2):
        for f in range(3):
            PB[half, :, f * 384 : f * 384 + 384] = pred[f : f + 1, half * 384 : half * 384 + 384]
    C1R[x * 8 + own_block] = PB[c]

    def send_piece(i):
        target, unused, b2 = plane_peer(i)
        send(PB.at[b2 % 2], C1R.at[x * 8 + own_block], ssem.at[13], rsem.at[13], target)

    for i in FAR_PLANE:
        send_piece(i)
    await_bytes(C1R.at[pl.ds(0, 31)], rsem.at[13])
    summed = jnp.sum(C1R[...], axis=0)
    C2S[...] = summed
    C2R[z] = summed

    def send_sum(i):
        target, unused = z_peer(i)
        send(C2S, C2R.at[z], ssem.at[14], rsem.at[14], target)

    for i in FAR_Z:
        send_sum(i)

    pl.when(has_below)(lambda: await_bytes(radR.at[2], rsem.at[7]))
    pl.when(has_above)(lambda: await_bytes(radR.at[3], rsem.at[8]))
    await_bytes(lonR.at[2], rsem.at[9])
    await_bytes(lonR.at[3], rsem.at[10])
    for f in range(3):
        for l in range(COLS):
            S1[f, l + 2, 15:16, :] = radR[2, f * 4 + l : f * 4 + l + 1, :]
            S1[f, l + 2, 12:13, :] = radR[3, f * 4 + l : f * 4 + l + 1, :]
    for l in range(COLS):
        X[0, l + 2, 14:15, :] = radR[2, 12 + l : 13 + l, :]
        X[0, l + 2, 13:14, :] = radR[3, 12 + l : 13 + l, :]
    for side, far, near in ((2, 0, 1), (3, 7, 6)):
        for f in range(3):
            S1[f, near, 0:ROWS, :] = lonR[side, f * ROWS : f * ROWS + ROWS, :]
            S1[f, near, ROWS:16, :] = jnp.zeros((16 - ROWS, NLAT), jnp.float32)
        X[0, far, 0:ROWS, :] = lonR[side, 36:48, :]
        X[0, far, ROWS:16, :] = jnp.zeros((16 - ROWS, NLAT), jnp.float32)
        X[0, near, ROWS:16, :] = lonR[side, 48:52, :]
    for p in range(8):
        E[p] = jnp.exp(X[0, p])
    for p in range(1, 7):
        QA[p] = edge_lat(E[p])
        QR[p] = edge_rad(E[p])
    for p in range(7):
        QO[p] = 0.1 / (E[p] + E[p + 1])
    for p in range(1, 7):
        slope = QR[p] * (wr_next - wr)
        AS[p] = wr + slope - last_row(slope)
        along = QA[p] * wr
        AA[p] = along
        AL[p] = last_lat(along)
    for p in range(7):
        AO[p] = QO[p] * wr
    for f in range(3):
        for p in range(1, 6):
            u, s, square = X[f + 1, p], S1[f, p], QO[p] * QO[p]
            UO[f, p] = square * (X[f + 1, p + 1] - u)
            SO[f, p] = square * wr * (S1[f, p + 1] - s)
            if p > 1:
                square = QA[p] * QA[p]
                UA[f, p] = square * (next_lat(u) - u)
                SA[f, p] = square * wr * (next_lat(s) - s)
                square = QR[p] * QR[p]
                UR[f, p] = square * (next_row(u) - u)
                SR[f, p] = square * (wr_next - wr) * (next_row(s) - s)
    for t in range(6):
        for p in range(8):
            TH[t * 128 : t * 128 + 128, p * 128 : p * 128 + 128] = KH[p * 128 : p * 128 + 128, t * 128 : t * 128 + 128].T
            TL[t * 128 : t * 128 + 128, p * 128 : p * 128 + 128] = KL[p * 128 : p * 128 + 128, t * 128 : t * 128 + 128].T

    record = jnp.where(c == 0, jnp.concatenate(tiles[0:3], axis=1), jnp.concatenate(tiles[3:6], axis=1))
    row_of = iota((8, 384), 0)
    weight = jnp.where(row_of < 3, pltpu.roll(record, 4, 0), 0.0)
    aim = pltpu.roll(record, 7, 0)

    await_bytes(C2R.at[pl.ds(0, 15)], rsem.at[14])
    total = jnp.sum(C2R[...], axis=0)
    predicted = jnp.concatenate(
        [total[:, f * 384 : f * 384 + 384] for f in range(3)] + [jnp.zeros((5, 384), jnp.float32)], axis=0
    )
    weighted = weight * (predicted - aim)
    squares = jnp.broadcast_to(jnp.sum(weighted * weighted, axis=0, keepdims=True), (8, 384))
    pulled = jnp.where(row_of == 3, squares, weight * weighted)
    C3S[...] = pulled[0:4]
    C3R[c] = pulled[0:4]
    send(C3S, C3R.at[c], ssem.at[15], rsem.at[15], device(y, z, 1 - c, x))
    await_bytes(C3R.at[0], rsem.at[15])
    pull = jnp.concatenate([C3R[0], C3R[1]], axis=1)
    pull = jnp.concatenate([pull, jnp.zeros((4, 768), jnp.float32)], axis=0)
    high, low = split(pull)
    both = jnp.concatenate([high, low], axis=0)

    first = dot(both, TH[...])
    adjoint = (first[0:8] + first[8:16] + dot(both, TL[...])[0:8]) * SCALE
    for f in range(3):
        for p in range(8):
            SD[f * 8 + p : f * 8 + p + 1, :] = adjoint[f : f + 1, p * 128 : p * 128 + 128]
    DR[x] = SD[...]

    def send_adjoint(i):
        target, unused = x_peer(i)
        send(SD, DR.at[x], ssem.at[16], rsem.at[16], target)

    repeat(1, 4, send_adjoint)
    misfit_ref[0] = jnp.sum(C3R[0, 3:4, :] + C3R[1, 3:4, :]) / (3.0 * 768.0)
    await_bytes(DR.at[pl.ds(0, 3)], rsem.at[16])

    faces_a = [jnp.zeros((16, NLAT), jnp.float32) for unused in range(8)]
    faces_r = [jnp.zeros((16, NLAT), jnp.float32) for unused in range(8)]
    faces_o = [jnp.zeros((16, NLAT), jnp.float32) for unused in range(8)]

    def spread(v, p):
        return jnp.broadcast_to(v[p : p + 1, :], (16, NLAT))

    for f in range(3):
        surface = jnp.concatenate([DR[band, f * 8 : f * 8 + 8, :] for band in range(4)], axis=1)
        step = next_lat(surface) - surface
        step_before = last_lat(step)
        beside = [spread(surface, p + 1) - spread(surface, p) for p in range(7)]
        a1 = [None] * 8
        for p in range(1, 7):
            a1[p] = (
                AS[p] * spread(surface, p) + AA[p] * spread(step, p) - AL[p] * spread(step_before, p)
                + AO[p] * beside[p] - AO[p - 1] * beside[p - 1]
            )
        for p in range(1, 6):
            faces_o[p] = faces_o[p] + UO[f, p] * (a1[p + 1] - a1[p]) + SO[f, p] * beside[p]
            if p > 1:
                faces_a[p] = faces_a[p] + UA[f, p] * (next_lat(a1[p]) - a1[p]) + SA[f, p] * spread(step, p)
                faces_r[p] = faces_r[p] + UR[f, p] * (next_row(a1[p]) - a1[p]) + SR[f, p] * spread(surface, p)
    for p in range(2, 6):
        along, upward = faces_a[p], faces_r[p]
        whole = (along + last_lat(along)) + (upward + last_row(upward)) + (faces_o[p] + faces_o[p - 1])
        result = 10.0 * E[p] * whole + 0.1 * X[0, p]
        grad_ref[:, p - 2, :] = result[0:ROWS, :]

    pl.when(has_above)(lambda: await_bytes(radS.at[0], ssem.at[0]))
    pl.when(has_below)(lambda: await_bytes(radS.at[1], ssem.at[1]))
    pl.when(has_above)(lambda: await_bytes(radS.at[2], ssem.at[7]))
    pl.when(has_below)(lambda: await_bytes(radS.at[3], ssem.at[8]))
    for k, ref in ((2, lonS.at[0, pl.ds(0, 48)]), (3, lonS.at[1, pl.ds(0, 48)]), (4, gathered.at[pl.ds(0, 7)]),
                   (5, sites.at[pl.ds(0, 7)]), (6, RB.at[pl.ds(0, 3)]), (9, lonS.at[2]), (10, lonS.at[3]),
                   (13, C1R.at[pl.ds(0, 31)]), (14, C2R.at[pl.ds(0, 15)]),
                   (15, C3S), (16, DR.at[pl.ds(0, 3)])):
        await_bytes(ref, ssem.at[k])


def body(logvisc, momentum, displacement, ice_history, load_steps, site_cells, observed, site_weight):
    f32 = jnp.float32
    vmem = pl.BlockSpec(memory_space=pltpu.VMEM)
    smem = pl.BlockSpec(memory_space=pltpu.SMEM)
    hbm = pl.BlockSpec(memory_space=pltpu.HBM)
    gradient, misfit = pl.pallas_call(
        kernel,
        out_shape=(
            pltpu.VMEM((ROWS, COLS, NLAT), f32),
            jax.ShapeDtypeStruct((1,), f32),
        ),
        in_specs=[hbm, hbm, hbm, smem, hbm, hbm, hbm],
        out_specs=(vmem, smem),
        scratch_shapes=[
            pltpu.VMEM((ROWS, COLS, NLAT), f32),
            pltpu.VMEM((3, ROWS, COLS, NLAT), f32),
            pltpu.VMEM((8, COLS, NLAT), f32),
            pltpu.VMEM((1, 12), jnp.int32),
            pltpu.VMEM((3, 12), f32),
            pltpu.VMEM((3, 12), f32),
            pltpu.VMEM((4, 8, 16, NLAT), f32),
            pltpu.VMEM((8, 16, NLAT), f32),
            pltpu.VMEM((3, 8, 16, NLAT), f32),
            pltpu.VMEM((8, 16, NLAT), f32),
            pltpu.VMEM((8, 16, NLAT), f32),
            pltpu.VMEM((8, 16, NLAT), f32),
            pltpu.VMEM((4, 16, NLAT), f32),
            pltpu.VMEM((4, 16, NLAT), f32),
            pltpu.VMEM((4, 56, NLAT), f32),
            pltpu.VMEM((4, 56, NLAT), f32),
            pltpu.VMEM((8, 128), f32),
            pltpu.VMEM((8, 8, 128), f32),
            pltpu.VMEM((8, 128), f32),
            pltpu.VMEM((8, 8, 128), f32),
            pltpu.VMEM((4, 24, 128), f32),
            pltpu.VMEM((4, 24, 128), f32),
            pltpu.VMEM((1024, 768), jnp.bfloat16),
            pltpu.VMEM((1024, 768), jnp.bfloat16),
            pltpu.VMEM((2, 1, 1152), f32),
            pltpu.VMEM((32, 1, 1152), f32),
            pltpu.VMEM((1, 1152), f32),
            pltpu.VMEM((16, 1, 1152), f32),
            pltpu.VMEM((4, 384), f32),
            pltpu.VMEM((2, 4, 384), f32),
            pltpu.VMEM((24, 128), f32),
            pltpu.VMEM((4, 24, 128), f32),
            pltpu.VMEM((768, 1024), jnp.bfloat16),
            pltpu.VMEM((768, 1024), jnp.bfloat16),
            pltpu.VMEM((8, 16, NLAT), f32),
            pltpu.VMEM((8, 16, NLAT), f32),
            pltpu.VMEM((8, 16, NLAT), f32),
            pltpu.VMEM((8, 16, NLAT), f32),
            pltpu.VMEM((3, 8, 16, NLAT), f32),
            pltpu.VMEM((3, 8, 16, NLAT), f32),
            pltpu.VMEM((3, 8, 16, NLAT), f32),
            pltpu.VMEM((3, 8, 16, NLAT), f32),
            pltpu.VMEM((3, 8, 16, NLAT), f32),
            pltpu.VMEM((3, 8, 16, NLAT), f32),
            pltpu.SemaphoreType.DMA((17,)),
            pltpu.SemaphoreType.DMA((17,)),
            pltpu.SemaphoreType.DMA((6,)),
        ],
        compiler_params=pltpu.CompilerParams(
            collective_id=0, has_side_effects=True, vmem_limit_bytes=62 * 1024 * 1024
        ),
    )(logvisc, displacement, ice_history, load_steps, site_cells.reshape(1, 12), observed, site_weight)
    half_momentum = momentum - 0.5 * gradient
    return logvisc + half_momentum, half_momentum, misfit


def solution(mesh):
    return jax.shard_map(
        body,
        mesh=mesh,
        in_specs=(
            P("rad", "lon", None),
            P("rad", "lon", None),
            P(None, "rad", "lon", None),
            P(None, "lon", None),
            P(),
            P("lon"),
            P(None, "lon"),
            P(None, "lon"),
        ),
        out_specs=(P("rad", "lon", None), P("rad", "lon", None), P()),
        check_vma=False,
    )
```

```python
import functools
import math

import jax
import jax.numpy as jnp
from jax import lax
from jax.experimental import pallas as pl
from jax.experimental.pallas import tpu as pltpu
from jax.sharding import PartitionSpec as P

MESH = pl.DeviceIdType.MESH
NR, NLON, NLAT = 96, 256, 512
ROWS = 12
COLS = 4
SCALE = 1.0 / math.sqrt(NLON * NLAT)
WAVE = [0.5 * (-1) ** k * (2.0 * math.pi) ** (2 * k + 1) / math.factorial(2 * k + 1) for k in range(6)]


def place():
    lon, rad = lax.axis_index("lon"), lax.axis_index("rad")
    return lon // 16, (rad // 4) * 8 + (lon // 2) % 8, lon % 2, rad % 4


def device(y, z, c, x):
    return (y * 16 + (z % 8) * 2 + c, (z // 8) * 4 + x)


def z_peer(i):
    y, z, c, x = place()
    z2 = (z + i) % 16
    return device(y, z2, c, x), z2


def plane_peer(i):
    y, z, c, x = place()
    x2, y2, c2 = (x + i % 4) % 4, (y + (i // 4) % 4) % 4, (c + i // 16) % 2
    return device(y2, z, c2, x2), x2, y2 * 2 + c2


def block_peer(i):
    y, z, c, x = place()
    y2, c2 = (y + i % 4) % 4, (c + i // 4) % 2
    return device(y2, z, c2, x), y2 * 2 + c2


def x_peer(i):
    y, z, c, x = place()
    x2 = (x + i) % 4
    return device(y, z, c, x2), x2


def repeat(first, last, step):
    for i in range(first, last):
        step(i)


def ring(offset, size):
    return min(offset % size, size - offset % size)


FAR_Z = sorted(range(1, 16), key=lambda i: -ring(i, 16))
NEAR_Z = [i for i in FAR_Z if ring(i, 16) <= 4]
FAR_PLANE = sorted(range(1, 32), key=lambda i: -(ring(i, 4) + ring(i // 4, 4) + 0.5 * (i // 16)))


def send(src, dst, ssem, rsem, target):
    pltpu.make_async_remote_copy(
        src_ref=src, dst_ref=dst, send_sem=ssem, recv_sem=rsem, device_id=target, device_id_type=MESH
    ).start()


def await_bytes(ref, sem):
    pltpu.make_async_copy(ref, ref, sem).wait()


def iota(shape, dim):
    return lax.broadcasted_iota(jnp.int32, shape, dim)


def next_lat(v):
    return pltpu.roll(v, NLAT - 1, v.ndim - 1)


def last_lat(v):
    return pltpu.roll(v, 1, v.ndim - 1)


def next_row(v):
    return pltpu.roll(v, 15, 0)


def last_row(v):
    return pltpu.roll(v, 1, 0)


def blocks_to_lanes(blocks):
    lane = iota((8, 128), 1)
    tiles = []
    for t in range(6):
        b = (128 * t) // 96
        first, second = 96 * b - 128 * t, 96 * (b + 1) - 128 * t
        low = pltpu.roll(blocks[b], first % 128, 1) if first % 128 else blocks[b]
        high = pltpu.roll(blocks[b + 1], second % 128, 1)
        tiles.append(jnp.where(lane < second, low, high))
    return tiles


def split(v):
    high = v.astype(jnp.bfloat16)
    return high, (v - high.astype(jnp.float32)).astype(jnp.bfloat16)


def kernel(
    lv_hbm, u_hbm, ice_hbm, steps_ref, cells_hbm, observed_hbm, weight_hbm,
    grad_ref, misfit_ref,
    lv_ref, u_ref, ice_ref, cells_ref, observed_ref, weight_ref,
    X, E, S1, QA, QO, QR, radS, radR, lonS, lonR,
    packet, gathered, block, sites, SB, RB, KH, KL,
    PB, C1R, C2S, C2R, C3S, C3R, SD, DR,
    TH, TL, AS, AA, AL, AO, UO, SO, UA, SA, UR, SR, ssem, rsem, isem,
):
    lon, rad = lax.axis_index("lon"), lax.axis_index("rad")
    y, z, c, x = place()
    own_block = y * 2 + c
    right, left = ((lon + 1) % 64, rad), ((lon + 63) % 64, rad)
    above, below = (lon, lax.min(rad + 1, 7)), (lon, lax.max(rad - 1, 0))

    barrier = pltpu.get_barrier_semaphore()

    def greet(target):
        pl.semaphore_signal(barrier, 1, device_id=target, device_id_type=MESH)

    has_above, has_below = rad < 7, rad > 0
    pl.when(has_above)(lambda: greet(above))
    pl.when(has_below)(lambda: greet(below))
    greet(right)
    greet(left)
    for i in NEAR_Z:
        greet(z_peer(i)[0])
    for i in FAR_PLANE:
        greet(plane_peer(i)[0])
    loads = [
        pltpu.make_async_copy(source, target, isem.at[k])
        for k, (source, target) in enumerate((
            (cells_hbm, cells_ref), (observed_hbm, observed_ref), (weight_hbm, weight_ref),
            (lv_hbm, lv_ref), (u_hbm, u_ref), (ice_hbm, ice_ref),
        ))
    ]
    for load in loads:
        load.start()
    for load in loads:
        load.wait()

    for f in range(4):
        for l in range(COLS):
            source = lv_ref[:, l, :] if f == 0 else u_ref[f - 1, :, l, :]
            X[f, l + 2, 0:ROWS, :] = source
            X[f, l + 2, ROWS:16, :] = jnp.zeros((16 - ROWS, NLAT), jnp.float32)
            radS[0, f * 4 + l : f * 4 + l + 1, :] = source[11:12, :]
            radS[1, f * 4 + l : f * 4 + l + 1, :] = source[0:1, :]
            if l == COLS - 1:
                lonS[0, f * ROWS : f * ROWS + ROWS, :] = source
            if l == 0:
                lonS[1, f * ROWS : f * ROWS + ROWS, :] = source
    packet[...] = jnp.zeros((8, 128), jnp.float32)
    packet[0:1, 0:12] = cells_ref[...].astype(jnp.float32)
    packet[1:4, 0:12] = observed_ref[...]
    packet[4:7, 0:12] = weight_ref[...]
    gathered[z % 8] = packet[...]
    nothing = jnp.zeros((16, NLAT), jnp.float32)

    @pl.when(rad == 7)
    def no_layer_above():
        radR[1] = nothing
        radR[3] = nothing

    @pl.when(rad == 0)
    def no_layer_below():
        radR[0] = nothing
        radR[2] = nothing

    pl.semaphore_wait(barrier, 41 + lax.min(rad, 1) + lax.min(7 - rad, 1))

    pl.when(has_above)(lambda: send(radS.at[0], radR.at[0], ssem.at[0], rsem.at[0], above))
    pl.when(has_below)(lambda: send(radS.at[1], radR.at[1], ssem.at[1], rsem.at[1], below))

    def send_edge(side):
        target = (lax.rem(lon + 65 - 2 * side, 64), rad)
        send(lonS.at[side, pl.ds(0, 48)], lonR.at[side, pl.ds(0, 48)], ssem.at[2 + side], rsem.at[2 + side], target)

    send_edge(1 - c)

    def send_record(i):
        target, unused = z_peer((i + 12) % 16)
        send(packet, gathered.at[z % 8], ssem.at[4], rsem.at[4], target)

    repeat(0, 4, send_record)
    repeat(5, 8, send_record)
    send_edge(c)

    row = iota((16, NLAT), 0)
    layer = jnp.where(row >= 14, row - 16, row)
    depth = (layer + rad * ROWS).astype(jnp.float32)
    wr = jnp.exp(4.0 * (depth - (NR - 1)) / NR)
    wr_next = jnp.exp(4.0 * (depth + 1.0 - (NR - 1)) / NR)
    own_row = row < ROWS
    wr_own = jnp.where(own_row, wr, 0.0)
    deep = layer + rad * ROWS
    face_ok = (row != 13) & (deep >= 0) & (deep < NR - 1)
    not_last = iota((16, NLAT), 1) < NLAT - 1
    is_top = jnp.where(rad == 7, 1.0, 0.0)

    def edge_lat(e):
        return jnp.where(not_last, 0.1 / (e + next_lat(e)), 0.0)

    for p in range(2, 6):
        E[p] = jnp.exp(X[0, p])
        QA[p] = edge_lat(E[p])
        for f in range(3):
            u = X[f + 1, p]
            flux = QA[p] * (next_lat(u) - u)
            S1[f, p] = u + (flux - last_lat(flux))
    for p in range(2, 5):
        QO[p] = 0.1 / (E[p] + E[p + 1])
        for f in range(3):
            flow = QO[p] * (X[f + 1, p + 1] - X[f + 1, p])
            S1[f, p] = S1[f, p] + flow
            S1[f, p + 1] = S1[f, p + 1] - flow

    await_bytes(gathered.at[pl.ds(0, 7)], rsem.at[4])
    record = gathered[0]
    for slot in range(1, 8):
        record = record + pltpu.roll(gathered[slot], 12 * slot, 1)
    block[...] = record
    sites[own_block] = record

    def send_block(i):
        target, unused = block_peer(i)
        send(block, sites.at[own_block], ssem.at[5], rsem.at[5], target)

    repeat(1, 8, send_block)

    await_bytes(lonR.at[0, pl.ds(0, 48)], rsem.at[2])
    await_bytes(lonR.at[1, pl.ds(0, 48)], rsem.at[3])
    for f in range(4):
        for side, p in ((0, 1), (1, 6)):
            X[f, p, 0:ROWS, :] = lonR[side, f * ROWS : f * ROWS + ROWS, :]
            X[f, p, ROWS:16, :] = jnp.zeros((16 - ROWS, NLAT), jnp.float32)
    pl.when(has_below)(lambda: await_bytes(radR.at[0], rsem.at[0]))
    pl.when(has_above)(lambda: await_bytes(radR.at[1], rsem.at[1]))
    for f in range(4):
        for l in range(COLS):
            X[f, l + 2, 15:16, :] = radR[0, f * 4 + l : f * 4 + l + 1, :]
            X[f, l + 2, 12:13, :] = radR[1, f * 4 + l : f * 4 + l + 1, :]

    def edge_rad(e):
        return jnp.where(face_ok, 0.1 / (e + next_row(e)), 0.0)

    for p in range(1, 7):
        E[p] = jnp.exp(X[0, p])
    for p in range(2, 6):
        QR[p] = edge_rad(E[p])
    for p in (1, 5):
        QO[p] = 0.1 / (E[p] + E[p + 1])
    load_1, load_2 = ice_ref[steps_ref[0]], ice_ref[steps_ref[1]]
    for f in range(3):
        for p in range(2, 6):
            u = X[f + 1, p]
            rise = QR[p] * (next_row(u) - u)
            total = S1[f, p] + (rise - last_row(rise))
            if p == 2:
                total = total + QO[1] * (X[f + 1, 1] - u)
            if p == 5:
                total = total + QO[5] * (X[f + 1, 6] - u)
            if f == 0:
                pressed = jnp.broadcast_to(load_1[p - 2 : p - 1, :], (16, NLAT)) * is_top
                total = total - jnp.where(row == ROWS - 1, pressed, 0.0)
            S1[f, p] = total

    columns = []
    for f in range(3):
        columns.append([jnp.zeros((1, NLAT), jnp.float32) for unused in range(8)])

    def column_sum(v):
        return jnp.sum(v, axis=0, keepdims=True)

    for p in range(2, 6):
        slope = QR[p] * (wr_next - wr)
        factor = jnp.where(own_row, wr + slope - last_row(slope), 0.0)
        along = wr_own * QA[p]
        for f in range(3):
            s = S1[f, p]
            flux = column_sum(along * (next_lat(s) - s))
            columns[f][p] = columns[f][p] + column_sum(factor * s) + (flux - last_lat(flux))
    for p in range(1, 6):
        across = wr_own * QO[p]
        for f in range(3):
            if p == 1:
                flow = column_sum(across * S1[f, 2])
            elif p == 5:
                flow = -column_sum(across * S1[f, 5])
            else:
                flow = column_sum(across * (S1[f, p + 1] - S1[f, p]))
            columns[f][p] = columns[f][p] + flow
            columns[f][p + 1] = columns[f][p + 1] - flow
    for p in range(2, 6):
        columns[0][p] = columns[0][p] - load_2[p - 2 : p - 1, :] * is_top
    for f in range(3):
        for p in range(8):
            for band in range(4):
                SB[band, f * 8 + p : f * 8 + p + 1, :] = columns[f][p][:, band * 128 : band * 128 + 128]
    RB[x] = SB[x]

    def send_band(i):
        target, x2 = x_peer(i)
        send(SB.at[x2], RB.at[x], ssem.at[6], rsem.at[6], target)

    repeat(1, 4, send_band)

    for f in range(3):
        for l in range(COLS):
            radS[2, f * 4 + l : f * 4 + l + 1, :] = S1[f, l + 2, 11:12, :]
            radS[3, f * 4 + l : f * 4 + l + 1, :] = S1[f, l + 2, 0:1, :]
    for l in range(COLS):
        radS[2, 12 + l : 13 + l, :] = X[0, l + 2, 10:11, :]
        radS[3, 12 + l : 13 + l, :] = X[0, l + 2, 1:2, :]
    for side, edge, inner in ((2, 5, 4), (3, 2, 3)):
        for f in range(3):
            lonS[side, f * ROWS : f * ROWS + ROWS, :] = S1[f, edge, 0:ROWS, :]
        lonS[side, 36:48, :] = X[0, inner, 0:ROWS, :]
        lonS[side, 48:52, :] = X[0, edge, ROWS:16, :]
        lonS[side, 52:56, :] = jnp.zeros((4, NLAT), jnp.float32)
    pl.when(has_above)(lambda: send(radS.at[2], radR.at[2], ssem.at[7], rsem.at[7], above))
    pl.when(has_below)(lambda: send(radS.at[3], radR.at[3], ssem.at[8], rsem.at[8], below))
    send(lonS.at[2], lonR.at[2], ssem.at[9], rsem.at[9], right)
    send(lonS.at[3], lonR.at[3], ssem.at[10], rsem.at[10], left)

    await_bytes(sites.at[pl.ds(0, 7)], rsem.at[5])
    tiles = blocks_to_lanes([sites[b] for b in range(8)])
    theta = (iota((128, 128), 0) + x * 128).astype(jnp.float32)
    theta = math.pi * (theta + 0.5) / NLAT
    cell_cos, cell_sin = jnp.cos(theta), jnp.sin(theta)
    plane_lon = (iota((8, 128), 0) + (lon * COLS - 2)).astype(jnp.float32)
    for t in range(6):
        cell = jnp.broadcast_to(tiles[t][0:1, :], (8, 128))
        site_lon = jnp.floor(cell * (1.0 / NLAT))
        site_theta = math.pi * (cell - NLAT * site_lon + 0.5) / NLAT
        up = jnp.cos(site_theta)
        side = jnp.sin(site_theta) * jnp.cos(2.0 * math.pi * (site_lon - plane_lon) / NLON)
        for p in range(8):
            cosine = cell_cos * up[0:1, :] + cell_sin * side[p : p + 1, :]
            chord = 2.0 - 2.0 * cosine
            turns = chord * (40.0 / (2.0 * math.pi))
            turns = 0.25 - jnp.abs(turns - jnp.round(turns))
            squared = turns * turns
            wave = jnp.full_like(squared, WAVE[5])
            for k in range(4, -1, -1):
                wave = wave * squared + WAVE[k]
            value = 1.0 / (1.0 + chord * 10.0) + wave * turns
            high, low = split(value)
            KH[p * 128 : p * 128 + 128, t * 128 : t * 128 + 128] = high
            KL[p * 128 : p * 128 + 128, t * 128 : t * 128 + 128] = low

    await_bytes(RB.at[pl.ds(0, 3)], rsem.at[6])
    band = (RB[0] + RB[1]) + (RB[2] + RB[3])
    place_of = iota((24, 128), 0) % 8
    wide = jnp.concatenate([jnp.where(place_of == p, band, 0.0) for p in range(1, 7)], axis=1)
    high, low = split(wide)
    dot = functools.partial(jnp.dot, preferred_element_type=jnp.float32)
    both = jnp.concatenate([high.astype(jnp.float32), low.astype(jnp.float32)], axis=0).astype(jnp.bfloat16)
    parts = dot(both, KH[128:896])
    parts = parts[0:24] + parts[24:48] + dot(high, KL[128:896])
    row8 = iota((8, 6 * 128), 0)
    pred = jnp.zeros((8, 6 * 128), jnp.float32)
    for f in range(3):
        summed = jnp.sum(parts[f * 8 : f * 8 + 8, :], axis=0, keepdims=True) * SCALE
        pred = jnp.where(row8 == f, jnp.broadcast_to(summed, pred.shape), pred)
    for half in range(2):
        for f in range(3):
            PB[half, :, f * 384 : f * 384 + 384] = pred[f : f + 1, half * 384 : half * 384 + 384]
    C1R[x * 8 + own_block] = PB[c]

    def send_piece(i):
        target, unused, b2 = plane_peer(i)
        send(PB.at[b2 % 2], C1R.at[x * 8 + own_block], ssem.at[13], rsem.at[13], target)

    for i in FAR_PLANE:
        send_piece(i)
    await_bytes(C1R.at[pl.ds(0, 31)], rsem.at[13])
    summed = jnp.sum(C1R[...], axis=0)
    C2S[...] = summed
    C2R[z] = summed

    def send_sum(i):
        target, unused = z_peer(i)
        send(C2S, C2R.at[z], ssem.at[14], rsem.at[14], target)

    for i in FAR_Z:
        send_sum(i)

    pl.when(has_below)(lambda: await_bytes(radR.at[2], rsem.at[7]))
    pl.when(has_above)(lambda: await_bytes(radR.at[3], rsem.at[8]))
    await_bytes(lonR.at[2], rsem.at[9])
    await_bytes(lonR.at[3], rsem.at[10])
    for f in range(3):
        for l in range(COLS):
            S1[f, l + 2, 15:16, :] = radR[2, f * 4 + l : f * 4 + l + 1, :]
            S1[f, l + 2, 12:13, :] = radR[3, f * 4 + l : f * 4 + l + 1, :]
    for l in range(COLS):
        X[0, l + 2, 14:15, :] = radR[2, 12 + l : 13 + l, :]
        X[0, l + 2, 13:14, :] = radR[3, 12 + l : 13 + l, :]
    for side, far, near in ((2, 0, 1), (3, 7, 6)):
        for f in range(3):
            S1[f, near, 0:ROWS, :] = lonR[side, f * ROWS : f * ROWS + ROWS, :]
            S1[f, near, ROWS:16, :] = jnp.zeros((16 - ROWS, NLAT), jnp.float32)
        X[0, far, 0:ROWS, :] = lonR[side, 36:48, :]
        X[0, far, ROWS:16, :] = jnp.zeros((16 - ROWS, NLAT), jnp.float32)
        X[0, near, ROWS:16, :] = lonR[side, 48:52, :]
    for p in range(8):
        E[p] = jnp.exp(X[0, p])
    for p in range(1, 7):
        QA[p] = edge_lat(E[p])
        QR[p] = edge_rad(E[p])
    for p in range(7):
        QO[p] = 0.1 / (E[p] + E[p + 1])
    for p in range(1, 7):
        slope = QR[p] * (wr_next - wr)
        AS[p] = wr + slope - last_row(slope)
        along = QA[p] * wr
        AA[p] = along
        AL[p] = last_lat(along)
    for p in range(7):
        AO[p] = QO[p] * wr
    for f in range(3):
        for p in range(1, 6):
            u, s, square = X[f + 1, p], S1[f, p], QO[p] * QO[p]
            UO[f, p] = square * (X[f + 1, p + 1] - u)
            SO[f, p] = square * wr * (S1[f, p + 1] - s)
            if p > 1:
                square = QA[p] * QA[p]
                UA[f, p] = square * (next_lat(u) - u)
                SA[f, p] = square * wr * (next_lat(s) - s)
                square = QR[p] * QR[p]
                UR[f, p] = square * (next_row(u) - u)
                SR[f, p] = square * (wr_next - wr) * (next_row(s) - s)
    for t in range(6):
        for p in range(8):
            TH[t * 128 : t * 128 + 128, p * 128 : p * 128 + 128] = KH[p * 128 : p * 128 + 128, t * 128 : t * 128 + 128].T
            TL[t * 128 : t * 128 + 128, p * 128 : p * 128 + 128] = KL[p * 128 : p * 128 + 128, t * 128 : t * 128 + 128].T

    record = jnp.where(c == 0, jnp.concatenate(tiles[0:3], axis=1), jnp.concatenate(tiles[3:6], axis=1))
    row_of = iota((8, 384), 0)
    weight = jnp.where(row_of < 3, pltpu.roll(record, 4, 0), 0.0)
    aim = pltpu.roll(record, 7, 0)

    await_bytes(C2R.at[pl.ds(0, 15)], rsem.at[14])
    total = jnp.sum(C2R[...], axis=0)
    predicted = jnp.concatenate(
        [total[:, f * 384 : f * 384 + 384] for f in range(3)] + [jnp.zeros((5, 384), jnp.float32)], axis=0
    )
    weighted = weight * (predicted - aim)
    squares = jnp.broadcast_to(jnp.sum(weighted * weighted, axis=0, keepdims=True), (8, 384))
    pulled = jnp.where(row_of == 3, squares, weight * weighted)
    C3S[...] = pulled[0:4]
    C3R[c] = pulled[0:4]
    send(C3S, C3R.at[c], ssem.at[15], rsem.at[15], device(y, z, 1 - c, x))
    await_bytes(C3R.at[0], rsem.at[15])
    pull = jnp.concatenate([C3R[0], C3R[1]], axis=1)
    pull = jnp.concatenate([pull, jnp.zeros((4, 768), jnp.float32)], axis=0)
    high, low = split(pull)
    both = jnp.concatenate([high, low], axis=0)

    first = dot(both, TH[...])
    adjoint = (first[0:8] + first[8:16] + dot(both, TL[...])[0:8]) * SCALE
    for f in range(3):
        for p in range(8):
            SD[f * 8 + p : f * 8 + p + 1, :] = adjoint[f : f + 1, p * 128 : p * 128 + 128]
    DR[x] = SD[...]

    def send_adjoint(i):
        target, unused = x_peer(i)
        send(SD, DR.at[x], ssem.at[16], rsem.at[16], target)

    repeat(1, 4, send_adjoint)
    misfit_ref[0] = jnp.sum(C3R[0, 3:4, :] + C3R[1, 3:4, :]) / (3.0 * 768.0)
    await_bytes(DR.at[pl.ds(0, 3)], rsem.at[16])

    faces_a = [jnp.zeros((16, NLAT), jnp.float32) for unused in range(8)]
    faces_r = [jnp.zeros((16, NLAT), jnp.float32) for unused in range(8)]
    faces_o = [jnp.zeros((16, NLAT), jnp.float32) for unused in range(8)]

    def spread(v, p):
        return jnp.broadcast_to(v[p : p + 1, :], (16, NLAT))

    for f in range(3):
        surface = jnp.concatenate([DR[band, f * 8 : f * 8 + 8, :] for band in range(4)], axis=1)
        step = next_lat(surface) - surface
        step_before = last_lat(step)
        beside = [spread(surface, p + 1) - spread(surface, p) for p in range(7)]
        a1 = [None] * 8
        for p in range(1, 7):
            a1[p] = (
                AS[p] * spread(surface, p) + AA[p] * spread(step, p) - AL[p] * spread(step_before, p)
                + AO[p] * beside[p] - AO[p - 1] * beside[p - 1]
            )
        for p in range(1, 6):
            faces_o[p] = faces_o[p] + UO[f, p] * (a1[p + 1] - a1[p]) + SO[f, p] * beside[p]
            if p > 1:
                faces_a[p] = faces_a[p] + UA[f, p] * (next_lat(a1[p]) - a1[p]) + SA[f, p] * spread(step, p)
                faces_r[p] = faces_r[p] + UR[f, p] * (next_row(a1[p]) - a1[p]) + SR[f, p] * spread(surface, p)
    for p in range(2, 6):
        along, upward = faces_a[p], faces_r[p]
        whole = (along + last_lat(along)) + (upward + last_row(upward)) + (faces_o[p] + faces_o[p - 1])
        result = 10.0 * E[p] * whole + 0.1 * X[0, p]
        grad_ref[:, p - 2, :] = result[0:ROWS, :]

    pl.when(has_above)(lambda: await_bytes(radS.at[0], ssem.at[0]))
    pl.when(has_below)(lambda: await_bytes(radS.at[1], ssem.at[1]))
    pl.when(has_above)(lambda: await_bytes(radS.at[2], ssem.at[7]))
    pl.when(has_below)(lambda: await_bytes(radS.at[3], ssem.at[8]))
    for k, ref in ((2, lonS.at[0, pl.ds(0, 48)]), (3, lonS.at[1, pl.ds(0, 48)]), (4, gathered.at[pl.ds(0, 7)]),
                   (5, sites.at[pl.ds(0, 7)]), (6, RB.at[pl.ds(0, 3)]), (9, lonS.at[2]), (10, lonS.at[3]),
                   (13, C1R.at[pl.ds(0, 31)]), (14, C2R.at[pl.ds(0, 15)]),
                   (15, C3S), (16, DR.at[pl.ds(0, 3)])):
        await_bytes(ref, ssem.at[k])


def body(logvisc, momentum, displacement, ice_history, load_steps, site_cells, observed, site_weight):
    f32 = jnp.float32
    vmem = pl.BlockSpec(memory_space=pltpu.VMEM)
    smem = pl.BlockSpec(memory_space=pltpu.SMEM)
    hbm = pl.BlockSpec(memory_space=pltpu.HBM)
    gradient, misfit = pl.pallas_call(
        kernel,
        out_shape=(
            pltpu.VMEM((ROWS, COLS, NLAT), f32),
            jax.ShapeDtypeStruct((1,), f32),
        ),
        in_specs=[hbm, hbm, hbm, smem, hbm, hbm, hbm],
        out_specs=(vmem, smem),
        scratch_shapes=[
            pltpu.VMEM((ROWS, COLS, NLAT), f32),
            pltpu.VMEM((3, ROWS, COLS, NLAT), f32),
            pltpu.VMEM((8, COLS, NLAT), f32),
            pltpu.VMEM((1, 12), jnp.int32),
            pltpu.VMEM((3, 12), f32),
            pltpu.VMEM((3, 12), f32),
            pltpu.VMEM((4, 8, 16, NLAT), f32),
            pltpu.VMEM((8, 16, NLAT), f32),
            pltpu.VMEM((3, 8, 16, NLAT), f32),
            pltpu.VMEM((8, 16, NLAT), f32),
            pltpu.VMEM((8, 16, NLAT), f32),
            pltpu.VMEM((8, 16, NLAT), f32),
            pltpu.VMEM((4, 16, NLAT), f32),
            pltpu.VMEM((4, 16, NLAT), f32),
            pltpu.VMEM((4, 56, NLAT), f32),
            pltpu.VMEM((4, 56, NLAT), f32),
            pltpu.VMEM((8, 128), f32),
            pltpu.VMEM((8, 8, 128), f32),
            pltpu.VMEM((8, 128), f32),
            pltpu.VMEM((8, 8, 128), f32),
            pltpu.VMEM((4, 24, 128), f32),
            pltpu.VMEM((4, 24, 128), f32),
            pltpu.VMEM((1024, 768), jnp.bfloat16),
            pltpu.VMEM((1024, 768), jnp.bfloat16),
            pltpu.VMEM((2, 1, 1152), f32),
            pltpu.VMEM((32, 1, 1152), f32),
            pltpu.VMEM((1, 1152), f32),
            pltpu.VMEM((16, 1, 1152), f32),
            pltpu.VMEM((4, 384), f32),
            pltpu.VMEM((2, 4, 384), f32),
            pltpu.VMEM((24, 128), f32),
            pltpu.VMEM((4, 24, 128), f32),
            pltpu.VMEM((768, 1024), jnp.bfloat16),
            pltpu.VMEM((768, 1024), jnp.bfloat16),
            pltpu.VMEM((8, 16, NLAT), f32),
            pltpu.VMEM((8, 16, NLAT), f32),
            pltpu.VMEM((8, 16, NLAT), f32),
            pltpu.VMEM((8, 16, NLAT), f32),
            pltpu.VMEM((3, 8, 16, NLAT), f32),
            pltpu.VMEM((3, 8, 16, NLAT), f32),
            pltpu.VMEM((3, 8, 16, NLAT), f32),
            pltpu.VMEM((3, 8, 16, NLAT), f32),
            pltpu.VMEM((3, 8, 16, NLAT), f32),
            pltpu.VMEM((3, 8, 16, NLAT), f32),
            pltpu.SemaphoreType.DMA((17,)),
            pltpu.SemaphoreType.DMA((17,)),
            pltpu.SemaphoreType.DMA((6,)),
        ],
        compiler_params=pltpu.CompilerParams(
            collective_id=0, has_side_effects=True, vmem_limit_bytes=62 * 1024 * 1024
        ),
    )(logvisc, displacement, ice_history, load_steps, site_cells.reshape(1, 12), observed, site_weight)
    half_momentum = momentum - 0.5 * gradient
    return logvisc + half_momentum, half_momentum, misfit


def solution(mesh):
    return jax.shard_map(
        body,
        mesh=mesh,
        in_specs=(
            P("rad", "lon", None),
            P("rad", "lon", None),
            P(None, "rad", "lon", None),
            P(None, "lon", None),
            P(),
            P("lon"),
            P(None, "lon"),
            P(None, "lon"),
        ),
        out_specs=(P("rad", "lon", None), P("rad", "lon", None), P()),
        check_vma=False,
    )
```
